128 devices in a mesh: seq: 64 (over x, y, z), ch: 2 (over core).
Axes of the slice: x: 4, y: 4, z: 4, core: 2. Of those that a mesh axis runs over, the one named last changes fastest.
Arguments:
- resident_samples: bfloat16 [1024, 196608], P('ch', 'seq'), may hold values from -6 to 6
- worker_sample_counts: int32 [64], P('seq'), may hold values from 1024 to 3072, as said below
- spaced_tap_kernel: bfloat16 [5, 3, 512, 1024], P(None, None, 'ch'), may hold values from -0.109375 to 0.109375
- restore_kernel: bfloat16 [5, 1024, 512], P(None, None, 'ch'), may hold values from -0.25 to 0.25
- shrinking_kernel: bfloat16 [2, 4, 1024, 1024], P(None, None, 'ch'), may hold values from -0.09375 to 0.09375
- embedding_projector: bfloat16 [64, 1024], P(None, 'ch'), may hold values from -0.1875 to 0.1875
- quantizer_dictionary: float32 [64, 2048], replicated, may hold values from -5 to 5
Outputs:
- sharpest_tier_result: bfloat16 [1024, 131072], P('ch', 'seq')
- latent: float32 [64, 8192], P(None, 'seq')
- nearest: float32 [8192], P('seq')
The draws below stay inside these ranges and needn't reach their ends.
Inputs may be any that keep to these rules, and one draw needn't show every extreme that they name: `worker_sample_counts`: the counts sum to 131072, and the sum of the counts of the loaders before loader d lies between d * 2048 and d * 2048 + 1024.
All inputs are finite; a program needn't handle non-finite values.
Results may differ from the reference program's by a relative error of at most 0.03.
Values may be sent and summed in bfloat16 or wider, within the bound.
A program may use at most 192 MiB of HBM per device.

```python
import jax
import jax.numpy as jnp
from jax import lax

CHANNEL_COUNT = 1024
RESIDUAL_HIDDEN = 512
EMB = 64
BINS = 2048
RESIDUAL_BLOCKS = 5
SHARD = 2048
HALF = 1024
CAP = 3072
FRAMES = 131072
N_SEQ = 64


def draw_worker_sample_counts(key, part):
    loaders = N_SEQ
    first_key, second_key = jax.random.split(jax.random.fold_in(key, 7))
    raised = jax.random.randint(first_key, (loaders + 1,), 0, HALF + 1)
    chosen = jax.random.randint(second_key, (), 1, loaders - 1)
    raised = raised.at[chosen - 1].set(0).at[chosen].set(HALF).at[chosen + 1].set(0)
    raised = raised.at[0].set(0).at[loaders].set(0)
    return (SHARD + raised[1:] - raised[:-1]).astype(jnp.int32)


def levels(own_key, extent, shards, smallest, top_value):
    def one(dim, parts):
        heights = jax.random.uniform(jax.random.fold_in(jax.random.fold_in(own_key, 6), dim), (parts,), jnp.float32, smallest / len(shards), top_value / len(shards))
        return jnp.repeat(jnp.exp(heights), extent[dim] // parts).reshape((-1,) + (1,) * (len(extent) - dim - 1))

    loudness = one(*shards[0])
    for cut in shards[1:]:
        loudness = loudness * one(*cut)
    return loudness


def bell_draw(rng, extent, scale, reach, pieces=(), kind=jnp.bfloat16):
    loudness = levels(rng, extent, pieces, -0.22, 0.18) if pieces else 1.0
    array = jax.random.normal(rng, extent, jnp.float32) * scale * loudness
    return jnp.minimum(jnp.maximum(array, -reach), reach).astype(kind)


def setup_inputs(seed: int = 0) -> dict:
    seeds = jax.random.split(jax.random.key(seed), 8)
    resident_samples = bell_draw(seeds[0], (CHANNEL_COUNT, N_SEQ * CAP), 1.0, 6.0, ((0, 2), (1, 64)))
    worker_sample_counts = draw_worker_sample_counts(jax.random.fold_in(seeds[7], 71), 0)
    spaced_tap_kernel = bell_draw(seeds[2], (RESIDUAL_BLOCKS, 3, RESIDUAL_HIDDEN, CHANNEL_COUNT), (3 * CHANNEL_COUNT) ** -0.5, 0.109375, ((2, 2),))
    restore_kernel = bell_draw(seeds[3], (RESIDUAL_BLOCKS, CHANNEL_COUNT, RESIDUAL_HIDDEN), RESIDUAL_HIDDEN ** -0.5, 0.25, ((2, 2),))
    shrinking_kernel = bell_draw(seeds[4], (2, 4, CHANNEL_COUNT, CHANNEL_COUNT), (4 * CHANNEL_COUNT) ** -0.5, 0.09375, ((2, 2),))
    embedding_projector = bell_draw(seeds[5], (EMB, CHANNEL_COUNT), CHANNEL_COUNT ** -0.5, 0.1875, ((1, 2),))
    quantizer_dictionary = bell_draw(seeds[6], (EMB, BINS), 1.0, 5.0, (), jnp.float32)
    return {"resident_samples": resident_samples, "worker_sample_counts": worker_sample_counts, "spaced_tap_kernel": spaced_tap_kernel, "restore_kernel": restore_kernel, "shrinking_kernel": shrinking_kernel, "embedding_projector": embedding_projector, "quantizer_dictionary": quantizer_dictionary}


dilation_rates = (1, 3, 1, 3, 3)


def apply_residual(hidden_state, w_one, w_two, dilation):
    frames = hidden_state.shape[1]
    activated = jnp.maximum(hidden_state, jnp.zeros((), hidden_state.dtype))
    extended = jnp.pad(activated, ((0, 0), (dilation, dilation)))
    summed = jnp.zeros((w_one.shape[1], frames), jnp.float32)
    for k in range(3):
        summed = summed + jnp.dot(w_one[k], extended[:, k * dilation:k * dilation + frames], preferred_element_type=jnp.float32)
    hidden = jnp.maximum(summed, 0.0).astype(jnp.bfloat16)
    update = jnp.dot(w_two, hidden, preferred_element_type=jnp.float32)
    return (hidden_state.astype(jnp.float32) + update).astype(jnp.bfloat16)


def skipping_contraction(hidden_state, weight_params):
    summed = jnp.zeros((weight_params.shape[1], hidden_state.shape[1] // 4), jnp.float32)
    for k in range(4):
        summed = summed + jnp.dot(weight_params[k], hidden_state[:, k::4], preferred_element_type=jnp.float32)
    return summed.astype(jnp.bfloat16)


def reference(resident_samples, worker_sample_counts, spaced_tap_kernel, restore_kernel, shrinking_kernel, embedding_projector, quantizer_dictionary):
    ends = jnp.cumsum(worker_sample_counts).astype(jnp.int32)
    starts = (ends - worker_sample_counts).astype(jnp.int32)
    position = jnp.arange(FRAMES, dtype=jnp.int32)
    loader = jnp.searchsorted(ends, position, side="right").astype(jnp.int32)
    columns = (loader * CAP + position - starts[loader]).astype(jnp.int32)
    frame_stream = jnp.take(resident_samples, columns, axis=1)
    sharpest_tier_result = apply_residual(frame_stream, spaced_tap_kernel[0], restore_kernel[0], dilation_rates[0])
    sharpest_tier_result = apply_residual(sharpest_tier_result, spaced_tap_kernel[1], restore_kernel[1], dilation_rates[1])
    intermediate_tier = skipping_contraction(sharpest_tier_result, shrinking_kernel[0])
    intermediate_tier = apply_residual(intermediate_tier, spaced_tap_kernel[2], restore_kernel[2], dilation_rates[2])
    intermediate_tier = apply_residual(intermediate_tier, spaced_tap_kernel[3], restore_kernel[3], dilation_rates[3])
    lowest_resolution_tier = skipping_contraction(intermediate_tier, shrinking_kernel[1])
    lowest_resolution_tier = apply_residual(lowest_resolution_tier, spaced_tap_kernel[4], restore_kernel[4], dilation_rates[4])
    latent = jnp.dot(embedding_projector, lowest_resolution_tier, preferred_element_type=jnp.float32)
    latent_sq = jnp.sum(latent * latent, axis=0)
    code_sq = jnp.sum(quantizer_dictionary * quantizer_dictionary, axis=0)
    products = jnp.dot(latent.T, quantizer_dictionary, precision=lax.Precision.HIGHEST)
    distance = latent_sq[:, None] + code_sq[None, :] - 2.0 * products
    nearest = jnp.min(distance, axis=1) / EMB
    return sharpest_tier_result, latent, nearest
```

```python
import jax
import jax.numpy as jnp
from jax import lax
from jax.experimental import pallas as pl
from jax.experimental.pallas import tpu as pltpu
from jax.sharding import PartitionSpec as P

MESH = pl.DeviceIdType.MESH
BF, F32, I32 = jnp.bfloat16, jnp.float32, jnp.int32
C, H, EMB, BINS, SHARD, CAP = 1024, 512, 64, 2048, 2048, 3072
T = 304
T2 = 80
HEAD = 24
PAD = 32
EDGE = 2 * T


def nt(a, b):
    return lax.dot_general(a, b, (((1,), (1,)), ((), ())), preferred_element_type=F32)


def nn(a, b):
    return jnp.dot(a, b, preferred_element_type=F32)


def iota(shape, dim):
    return lax.broadcasted_iota(I32, shape, dim)


def ones_where(mask):
    return jnp.where(mask, 1.0, 0.0).astype(BF)


def kernel(
    cnt_ref, res_hbm, w1_hbm, w2_hbm, dn_hbm, pj_hbm, cb_hbm,
    out_hbm, lat_ref, near_ref,
    res, w1, w2, dn, pj, cb, cbk, counts, place, edge, send_r, send_rr, shift, x, a, pb, carry, hid, y32, z, u, v, ot,
    msg, msg_peer, msg_left,
    lsem, rsem, wsend, wrecv, csend, crecv, esend, erecv, hsend, hrecv, olocal, osend, opeer, oleft, msend, mrecv,
):
    s, c = lax.axis_index("seq"), lax.axis_index("ch")
    n_seq = lax.axis_size("seq")
    right, left = lax.rem(s + 1, n_seq), lax.rem(s + n_seq - 1, n_seq)
    other = 1 - c
    peer = {"seq": s, "ch": other}
    rounds = ((lax.rem(s, 4), 1), (lax.rem(s // 4, 4), 4), (s // 16, 16))
    last = (s == n_seq - 1) & (c == 1)

    def remote(src, dst, send, recv, where):
        return pltpu.make_async_remote_copy(
            src_ref=src, dst_ref=dst, send_sem=send, recv_sem=recv, device_id=where, device_id_type=MESH
        )

    def weight(i, on):
        if i < 15:
            b, k = divmod(i, 3)
            tap = k + (1 - on) * (2 - 2 * k)
            return w1_hbm.at[b, k], w1.at[b, pl.ds(pl.multiple_of(512 * tap + 256 * c, 256), 256)]
        if i < 20:
            return w2_hbm.at[i - 15], w2.at[i - 15, :, pl.ds(pl.multiple_of(256 * c, 256), 256)]
        if i < 28:
            l, k = divmod(i - 20, 4)
            tap = k + (1 - on) * (3 - 2 * k)
            return dn_hbm.at[l, k], dn.at[
                l, pl.ds(pl.multiple_of(512 * c, 512), 512), pl.ds(pl.multiple_of(1024 * tap, 1024), 1024)
            ]
        return pj_hbm, pj.at[pl.ds(0, EMB), pl.ds(pl.multiple_of(512 * c, 512), 512)]

    def weight_local(i):
        return pltpu.make_async_copy(*weight(i, c), lsem.at[i])

    def weight_remote(i):
        return remote(*weight(i, other), wsend.at[i], wrecv.at[i], peer)

    def block_weights(b):
        return [3 * b, 3 * b + 1, 3 * b + 2, 15 + b]

    def down_weights(l):
        return [20 + 4 * l + k for k in range(4)]

    def need(items):
        for i in items:
            weight_local(i).wait()
            weight_remote(i).wait_recv()

    groups = [
        block_weights(0) + block_weights(1),
        down_weights(0) + block_weights(2),
        block_weights(3) + down_weights(1) + block_weights(4) + [28],
    ]
    load_res = [
        pltpu.make_async_copy(res_hbm.at[:, pl.ds(128 * k, 128)], res.at[k], rsem.at[k]) for k in range(CAP // 128)
    ]
    load_cb = pltpu.make_async_copy(cb_hbm, cb, lsem.at[30])
    for copy in load_res:
        copy.start()
    load_cb.start()

    barrier = pltpu.get_barrier_semaphore()
    greeted = [peer] + [{"seq": chip, "ch": core} for chip in (left, right) for core in (0, 1)]
    partners = [[], [], []]
    for dim, (at, stride) in enumerate(rounds):
        for q in (1, 2, 3):
            j = lax.rem(at + q, 4)
            partners[dim].append((j, {"seq": s + (j - at) * stride, "ch": c}))
            greeted.append(partners[dim][-1][1])
    for where in greeted:
        pl.semaphore_signal(barrier, inc=1, device_id=where, device_id_type=MESH)

    cnt = cnt_ref[0]
    x[0:PAD, :] = jnp.zeros((PAD, C), BF)
    pb[...] = jnp.zeros(pb.shape, F32)
    carry[...] = jnp.zeros(carry.shape, F32)

    def picked(first, sign):
        lowest = jnp.maximum(jnp.minimum(first, first + sign * (T - 1)), 0)
        tile = jnp.minimum(lax.shift_right_logical(lowest, 7), CAP // 128 - 4)
        column = 128 * tile + iota((T, 512), 1)
        pick = ones_where((column == first + sign * iota((T, 512), 0)) & (column < cnt))
        found = jnp.concatenate([res[tile + q] for q in range(4)], axis=1)
        return nt(pick, found).astype(BF)

    def count_round(dim, value):
        at = rounds[dim][0]
        counts[dim, at] = value
        copies = []
        for q, (j, where) in enumerate(partners[dim]):
            copies.append(
                remote(counts.at[dim, at], counts.at[dim, at], csend.at[dim, q], crecv.at[dim, at], where)
            )
            copies[-1].start()
        return copies

    def count_sums(dim):
        at = rounds[dim][0]
        for q, (j, where) in enumerate(partners[dim]):
            remote(counts.at[dim, j], counts.at[dim, j], csend.at[dim, q], crecv.at[dim, j], where).wait_recv()
        before, total = jnp.zeros((8, 128), I32), jnp.zeros((8, 128), I32)
        for j in range(4):
            value = counts[dim, j]
            total = total + value
            before = before + jnp.where(j < at, value, 0)
        return before, total

    half_c = pl.ds(pl.multiple_of(512 * c, 512), 512)
    sends = []

    def send_edges(m):
        for q, (buffer, where) in enumerate(
            ((send_r, {"seq": right, "ch": 0}), (send_rr, {"seq": left, "ch": 1}))
        ):
            copy = remote(buffer.at[m], edge.at[m, :, half_c], esend.at[m, q], erecv.at[m, c], where)
            copy.start()
            sends.append(copy)

    for copy in load_res:
        copy.wait()
    for i in groups[0]:
        weight_local(i).start()
    pl.semaphore_wait(barrier, len(greeted))
    sends += count_round(0, jnp.full((8, 128), cnt, I32))
    send_r[0] = picked(cnt - 1, -1)
    send_rr[0] = picked(jnp.int32(0), 1)
    send_edges(0)
    before, total = count_sums(0)
    sends += count_round(1, total)
    for i in groups[0]:
        sends.append(weight_remote(i))
        sends[-1].start()
    send_r[1] = picked(cnt - 1 - T, -1)
    send_rr[1] = picked(jnp.int32(T), 1)
    send_edges(1)
    more, total = count_sums(1)
    before = before + more
    sends += count_round(2, total)
    for g in (1, 2):
        for i in groups[g]:
            weight_local(i).start()
    more, total = count_sums(2)
    place[...] = before + more - SHARD * s
    offset = place[0, 0]
    gap = jnp.where(c == 0, SHARD // 2 - offset, offset + cnt - SHARD)

    def window(core, n):
        sign = 2 * core - 1
        first = jnp.where(core == 1, 1440, 1631) + sign * T * n - offset
        return picked(first, sign)

    def to_peer(h):
        rows = pl.ds(PAD + EDGE * h, EDGE)
        return remote(shift.at[h], x.at[rows, half_c], hsend.at[h], hrecv.at[h], peer)

    for h in (0, 1):

        def shifted(n, _):
            shift[h, pl.ds(pl.multiple_of(T * n, 16), T), :] = window(other, 2 * h + n)
            return 0

        lax.fori_loop(0, 2, shifted, 0)
        sends.append(to_peer(h))
        sends[-1].start()

    def placed(n, _):
        x[pl.ds(pl.multiple_of(PAD + T * n, 16), T), half_c] = window(c, n)
        return 0

    lax.fori_loop(0, 4, placed, 0)
    for i in groups[1]:
        sends.append(weight_remote(i))
        sends[-1].start()

    def block(ref, at, rows, b, dilation, lag, bound, wide_at):
        def tap(n, _):
            lanes = pl.ds(pl.multiple_of(256 * n, 256), 256)
            pb[HEAD : HEAD + rows, lanes] = nt(a[:rows, :], w1[b, lanes, :])
            return 0

        lax.fori_loop(0, 6, tap, 0)

        def hide(n, _):
            here = HEAD - lag

            def product(k, start):
                return pb[start : start + rows, pl.ds(pl.multiple_of(512 * k + 128 * n, 128), 128)]

            p0, p1, p2 = product(0, here - dilation), product(1, here), product(2, here + dilation)
            if bound is not None:
                t = iota((rows, 128), 0) - jnp.where(last, bound, 1 << 20)
                p0 = jnp.where((t >= 0) & (t < dilation), 0.0, p0)
                p2 = jnp.where((t < 0) & (t >= -dilation), 0.0, p2)
            hid[:rows, pl.ds(pl.multiple_of(128 * n, 128), 128)] = jnp.maximum(p0 + p1 + p2, 0.0).astype(BF)
            return 0

        lax.fori_loop(0, 4, hide, 0)
        if lag:
            carry[b] = pb[rows : rows + HEAD, :]

        def back(n, _):
            lanes = pl.ds(pl.multiple_of(256 * n, 256), 256)
            update = nt(hid[:rows, :], w2[b, lanes, :])
            new = (ref[at : at + rows, lanes].astype(F32) + update).astype(BF)
            ref[at : at + rows, lanes] = new
            if wide_at is not None:
                for q in (0, 1):
                    y32[2 * n + q, wide_at : wide_at + rows, :] = new[:, 128 * q : 128 * (q + 1)].astype(F32)
            return 0

        lax.fori_loop(0, 4, back, 0)

    def out_tile(i):
        r, q = iota((256, 256), 0), iota((256, 256), 1)
        order = ones_where(jnp.where(c == 0, 255 - r, r) == q)
        same = ones_where(r == q)

        def turn(n, _):
            lanes = pl.ds(pl.multiple_of(256 * n, 256), 256)
            rows = nn(order, x[PAD + 96 + 256 * i : PAD + 352 + 256 * i, lanes]).astype(BF)
            ot[i, lanes, :] = nt(same, rows).astype(BF)
            return 0

        lax.fori_loop(0, 4, turn, 0)

    def half(core):
        return pl.ds(pl.multiple_of(512 * core, 512), 512)

    def own_tile(i, start):
        columns = pl.ds(pl.multiple_of(start, 256), 256)
        return (
            pltpu.make_async_copy(ot.at[i, half(c)], out_hbm.at[:, columns], olocal.at[i]),
            remote(ot.at[i, half(other)], out_hbm.at[:, columns], osend.at[i, 0], opeer.at[i], peer),
        )

    def next_tile(i):
        columns = pl.ds(256 * (i - 2), 256)
        return [
            remote(
                ot.at[i, pl.ds(512 * core, 512)],
                out_hbm.at[:, columns],
                osend.at[i, core],
                oleft.at[i - 2],
                {"seq": right, "ch": core},
            )
            for core in (0, 1)
        ]

    def emit(i):
        out_tile(i)
        if i < 2:
            for copy in own_tile(i, jnp.where(c == 0, 1280 - 256 * i, 1536 + 256 * i)):
                copy.start()
        else:

            @pl.when(c == 0)
            def _():
                for copy in own_tile(i, 1280 - 256 * i):
                    copy.start()

            @pl.when(c == 1)
            def _():
                for copy in next_tile(i):
                    copy.start()

    for n in range(4):
        at = PAD + T * n
        if n % 2 == 0:
            to_peer(n // 2).wait_recv()
        if n >= 2:
            m = n - 2
            for core in (0, 1):
                remote(
                    send_r.at[m], edge.at[m, :, pl.ds(512 * core, 512)], esend.at[m, 0], erecv.at[m, core],
                    {"seq": right, "ch": 0},
                ).wait_recv()
            picks = [
                ones_where(T * e + iota((T, T), 1) == T * m + iota((T, T), 0) - gap) for e in range(m + 1)
            ]

            def fill(q, _):
                lanes = pl.ds(pl.multiple_of(256 * q, 256), 256)
                total = x[at : at + T, lanes].astype(F32)
                for e in range(m + 1):
                    total = total + nn(picks[e], edge[e, :, lanes])
                x[at : at + T, lanes] = total.astype(BF)
                return 0

            lax.fori_loop(0, 4, fill, 0)
        for b, dilation in ((0, 1), (1, 3)):
            if n == 0:
                need(block_weights(b))
            start = at - 16 * b
            a[...] = jnp.maximum(x[start : start + T, :], jnp.zeros((), BF))
            pb[0:HEAD, :] = carry[b]
            bound = EDGE - (T * n - 16 * b - 16) if n == 2 else None
            block(x, start - 16, T, b, dilation, 16, bound, T * n if b == 1 else None)
        if n == 0:
            for i in groups[2]:
                sends.append(weight_remote(i))
                sends[-1].start()
        for i in ((), (0,), (1, 2), (3,))[n]:
            emit(i)

    def fold(rows):
        def one(n, _):
            for k in range(4):
                lanes = pl.ds(pl.multiple_of(1024 * k + 128 * n, 128), 128)
                z[:rows, lanes] = y32[n, pl.ds(k, rows, stride=4), :].astype(BF)
            return 0

        lax.fori_loop(0, 8, one, 0)

    fold(T)
    need(down_weights(0))

    def down(l, rows, to):
        def one(n, _):
            lanes = pl.ds(pl.multiple_of(256 * n, 256), 256)
            to[:, lanes] = nt(z[:rows, :], dn[l, lanes, :]).astype(BF)
            return 0

        lax.fori_loop(0, 4, one, 0)

    down(0, T, u)
    for b, dilation in ((2, 1), (3, 3)):
        need(block_weights(b))
        a[...] = jnp.maximum(u[...], jnp.zeros((), BF))
        block(u, 0, T, b, dilation, 0, 160, 0 if b == 3 else None)

    fold(T2)
    need(down_weights(1))
    down(1, T2, v)
    need(block_weights(4))
    a[:T2, :] = jnp.maximum(v[...], jnp.zeros((), BF))
    block(v, 0, T2, 4, 3, 0, 40, None)

    need([28])
    load_cb.wait()
    pj[EMB : 2 * EMB, :] = pj[0:EMB, :]
    pj[2 * EMB : 3 * EMB, :] = pj[0:EMB, :]
    book = cb[...]
    book_hi = book.astype(BF)
    cbk[0:EMB, :] = book_hi
    cbk[EMB : 2 * EMB, :] = book_hi
    cbk[2 * EMB : 3 * EMB, :] = (book - book_hi.astype(F32)).astype(BF)
    book_sq = jnp.sum(book * book, axis=0, keepdims=True)
    frame, row = iota((128, T2), 0), iota((128, T2), 1)
    spot = jnp.where(c == 0, 103 - row, lax.rem(88 + row, 128))
    coarse = nn(ones_where((spot == frame) & (row >= 8) & (row < 72)), v[...]).astype(BF)
    latent = nt(pj[0:EMB, :], coarse)
    thrice = nt(coarse, pj[...])
    hi = thrice.astype(BF)
    lo = (thrice - hi.astype(F32)).astype(BF)
    lane = iota((128, 3 * EMB), 1)
    lhs = jnp.where((lane >= EMB) & (lane < 2 * EMB), lo, hi)
    nearest = jnp.full((128, 1), jnp.inf, F32)
    for q in range(4):
        columns = slice(512 * q, 512 * (q + 1))
        distance = book_sq[:, columns] - 2.0 * nn(lhs, cbk[:, columns])
        nearest = jnp.minimum(nearest, jnp.min(distance, axis=1, keepdims=True))
    diagonal = iota((128, 128), 0) == iota((128, 128), 1)
    nearest = jnp.sum(jnp.where(diagonal, nearest, 0.0), axis=0, keepdims=True)
    nearest = (nearest + jnp.sum(latent * latent, axis=0, keepdims=True)) * (1.0 / EMB)
    msg[0:EMB, :] = latent
    msg[EMB : EMB + 8, :] = jnp.broadcast_to(nearest, (8, 128))
    tell_peer = remote(msg, msg_peer, msend.at[0], mrecv.at[0], peer)
    tell_next = [
        remote(msg, msg_left, msend.at[1 + core], mrecv.at[1], {"seq": right, "ch": core}) for core in (0, 1)
    ]
    tell_peer.start()

    @pl.when(c == 1)
    def _():
        for copy in tell_next:
            copy.start()

    tell_peer.wait_recv()
    tell_next[0].wait_recv()
    lane = iota((EMB + 8, 128), 1)
    own = jnp.where(c == 0, msg[...], msg_peer[...])
    late = jnp.where(c == 0, msg_peer[...], msg[...])
    whole = jnp.where(lane < 32, msg_left[...], jnp.where(lane < 96, own, late))
    lat_ref[...] = whole[0:EMB, :]
    near_ref[...] = whole[EMB : EMB + 8, :]

    tell_peer.wait_send()
    for copy in sends:
        copy.wait_send()
    for i in (0, 1):
        mine, theirs = own_tile(i, jnp.where(c == 0, 1280 - 256 * i, 1536 + 256 * i))
        mine.wait()
        theirs.wait()
        next_tile(2 + i)[0].wait_recv()

    @pl.when(c == 0)
    def _():
        for i in (2, 3):
            mine, theirs = own_tile(i, 1280 - 256 * i)
            mine.wait()
            theirs.wait_send()

    @pl.when(c == 1)
    def _():
        for copy in tell_next:
            copy.wait_send()
        for i in (2, 3):
            own_tile(i, 1280 - 256 * i)[1].wait_recv()
            for copy in next_tile(i):
                copy.wait_send()


def on_device(samples, sample_counts, spaced, restore, shrinking, projector, dictionary):
    hbm = pl.BlockSpec(memory_space=pltpu.HBM)
    vmem = pl.BlockSpec(memory_space=pltpu.VMEM)
    dma = pltpu.SemaphoreType.DMA
    sharpest, latent, nearest = pl.pallas_call(
        kernel,
        out_shape=(
            jax.ShapeDtypeStruct((H, SHARD), BF),
            jax.ShapeDtypeStruct((EMB, 128), F32),
            jax.ShapeDtypeStruct((8, 128), F32),
        ),
        in_specs=[pl.BlockSpec(memory_space=pltpu.SMEM)] + [hbm] * 6,
        out_specs=(hbm, vmem, vmem),
        scratch_shapes=[
            pltpu.VMEM((CAP // 128, H, 128), BF),
            pltpu.VMEM((5, 3 * H, C), BF),
            pltpu.VMEM((5, C, H), BF),
            pltpu.VMEM((2, C, 4 * C), BF),
            pltpu.VMEM((3 * EMB, C), BF),
            pltpu.VMEM((EMB, BINS), F32),
            pltpu.VMEM((3 * EMB, BINS), BF),
            pltpu.VMEM((3, 4, 8, 128), I32),
            pltpu.VMEM((8, 128), I32),
            pltpu.VMEM((2, T, C), BF),
            pltpu.VMEM((2, T, H), BF),
            pltpu.VMEM((2, T, H), BF),
            pltpu.VMEM((2, EDGE, H), BF),
            pltpu.VMEM((PAD + 4 * T, C), BF),
            pltpu.VMEM((T, C), BF),
            pltpu.VMEM((HEAD + T + 8, 3 * H), F32),
            pltpu.VMEM((2, HEAD, 3 * H), F32),
            pltpu.VMEM((T, H), BF),
            pltpu.VMEM((8, 4 * T, 128), F32),
            pltpu.VMEM((T, 4 * C), BF),
            pltpu.VMEM((T, C), BF),
            pltpu.VMEM((T2, C), BF),
            pltpu.VMEM((4, C, 256), BF),
            pltpu.VMEM((EMB + 8, 128), F32),
            pltpu.VMEM((EMB + 8, 128), F32),
            pltpu.VMEM((EMB + 8, 128), F32),
            dma((31,)),
            dma((CAP // 128,)),
            dma((29,)),
            dma((29,)),
            dma((3, 3)),
            dma((3, 4)),
            dma((2, 2)),
            dma((2, 2)),
            dma((2,)),
            dma((2,)),
            dma((4,)),
            dma((4, 2)),
            dma((4,)),
            dma((2,)),
            dma((3,)),
            dma((2,)),
        ],
        compiler_params=pltpu.CompilerParams(
            collective_id=0, has_side_effects=True, vmem_limit_bytes=63 * 2**20
        ),
        name="encoder",
    )(sample_counts, samples, spaced, restore, shrinking, projector, dictionary)
    return sharpest, latent, nearest[0]


def solution(mesh):
    return jax.shard_map(
        on_device,
        mesh=mesh,
        in_specs=(
            P("ch", "seq"),
            P("seq"),
            P(None, None, "ch", None),
            P(None, None, "ch"),
            P(None, None, "ch", None),
            P(None, "ch"),
            P(),
        ),
        out_specs=(P("ch", "seq"), P(None, "seq"), P("seq")),
        check_vma=False,
    )
```

```python
import jax
import jax.numpy as jnp
from jax import lax
from jax.experimental import pallas as pl
from jax.experimental.pallas import tpu as pltpu
from jax.sharding import PartitionSpec as P

MESH = pl.DeviceIdType.MESH
BF, F32, I32 = jnp.bfloat16, jnp.float32, jnp.int32
C, H, EMB, BINS, SHARD, CAP = 1024, 512, 64, 2048, 2048, 3072
T = 304
T2 = 80
HEAD = 24
PAD = 32
EDGE = 2 * T


def nt(a, b):
    return lax.dot_general(a, b, (((1,), (1,)), ((), ())), preferred_element_type=F32)


def nn(a, b):
    return jnp.dot(a, b, preferred_element_type=F32)


def iota(shape, dim):
    return lax.broadcasted_iota(I32, shape, dim)


def ones_where(mask):
    return jnp.where(mask, 1.0, 0.0).astype(BF)


def kernel(
    cnt_ref, res_hbm, w1_hbm, w2_hbm, dn_hbm, pj_hbm, cb_hbm,
    out_hbm, lat_ref, near_ref,
    res, w1, w2, dn, pj, cb, cbk, counts, place, edge, send_r, send_rr, shift, x, a, pb, carry, hid, y32, z, u, v, ot,
    msg, msg_peer, msg_left,
    lsem, rsem, wsend, wrecv, csend, crecv, esend, erecv, hsend, hrecv, olocal, osend, opeer, oleft, msend, mrecv,
):
    s, c = lax.axis_index("seq"), lax.axis_index("ch")
    n_seq = lax.axis_size("seq")
    right, left = lax.rem(s + 1, n_seq), lax.rem(s + n_seq - 1, n_seq)
    other = 1 - c
    peer = {"seq": s, "ch": other}
    rounds = ((lax.rem(s, 4), 1), (lax.rem(s // 4, 4), 4), (s // 16, 16))
    last = (s == n_seq - 1) & (c == 1)

    def remote(src, dst, send, recv, where):
        return pltpu.make_async_remote_copy(
            src_ref=src, dst_ref=dst, send_sem=send, recv_sem=recv, device_id=where, device_id_type=MESH
        )

    def weight(i, on):
        if i < 15:
            b, k = divmod(i, 3)
            tap = k + (1 - on) * (2 - 2 * k)
            return w1_hbm.at[b, k], w1.at[b, pl.ds(pl.multiple_of(512 * tap + 256 * c, 256), 256)]
        if i < 20:
            return w2_hbm.at[i - 15], w2.at[i - 15, :, pl.ds(pl.multiple_of(256 * c, 256), 256)]
        if i < 28:
            l, k = divmod(i - 20, 4)
            tap = k + (1 - on) * (3 - 2 * k)
            return dn_hbm.at[l, k], dn.at[
                l, pl.ds(pl.multiple_of(512 * c, 512), 512), pl.ds(pl.multiple_of(1024 * tap, 1024), 1024)
            ]
        return pj_hbm, pj.at[pl.ds(0, EMB), pl.ds(pl.multiple_of(512 * c, 512), 512)]

    def weight_local(i):
        return pltpu.make_async_copy(*weight(i, c), lsem.at[i])

    def weight_remote(i):
        return remote(*weight(i, other), wsend.at[i], wrecv.at[i], peer)

    def block_weights(b):
        return [3 * b, 3 * b + 1, 3 * b + 2, 15 + b]

    def down_weights(l):
        return [20 + 4 * l + k for k in range(4)]

    def need(items):
        for i in items:
            weight_local(i).wait()
            weight_remote(i).wait_recv()

    groups = [
        block_weights(0) + block_weights(1),
        down_weights(0) + block_weights(2),
        block_weights(3) + down_weights(1) + block_weights(4) + [28],
    ]
    load_res = [
        pltpu.make_async_copy(res_hbm.at[:, pl.ds(128 * k, 128)], res.at[k], rsem.at[k]) for k in range(CAP // 128)
    ]
    load_cb = pltpu.make_async_copy(cb_hbm, cb, lsem.at[30])
    for copy in load_res:
        copy.start()
    load_cb.start()

    barrier = pltpu.get_barrier_semaphore()
    greeted = [peer] + [{"seq": chip, "ch": core} for chip in (left, right) for core in (0, 1)]
    partners = [[], [], []]
    for dim, (at, stride) in enumerate(rounds):
        for q in (1, 2, 3):
            j = lax.rem(at + q, 4)
            partners[dim].append((j, {"seq": s + (j - at) * stride, "ch": c}))
            greeted.append(partners[dim][-1][1])
    for where in greeted:
        pl.semaphore_signal(barrier, inc=1, device_id=where, device_id_type=MESH)

    cnt = cnt_ref[0]
    x[0:PAD, :] = jnp.zeros((PAD, C), BF)
    pb[...] = jnp.zeros(pb.shape, F32)
    carry[...] = jnp.zeros(carry.shape, F32)

    def picked(first, sign):
        lowest = jnp.maximum(jnp.minimum(first, first + sign * (T - 1)), 0)
        tile = jnp.minimum(lax.shift_right_logical(lowest, 7), CAP // 128 - 4)
        column = 128 * tile + iota((T, 512), 1)
        pick = ones_where((column == first + sign * iota((T, 512), 0)) & (column < cnt))
        found = jnp.concatenate([res[tile + q] for q in range(4)], axis=1)
        return nt(pick, found).astype(BF)

    def count_round(dim, value):
        at = rounds[dim][0]
        counts[dim, at] = value
        copies = []
        for q, (j, where) in enumerate(partners[dim]):
            copies.append(
                remote(counts.at[dim, at], counts.at[dim, at], csend.at[dim, q], crecv.at[dim, at], where)
            )
            copies[-1].start()
        return copies

    def count_sums(dim):
        at = rounds[dim][0]
        for q, (j, where) in enumerate(partners[dim]):
            remote(counts.at[dim, j], counts.at[dim, j], csend.at[dim, q], crecv.at[dim, j], where).wait_recv()
        before, total = jnp.zeros((8, 128), I32), jnp.zeros((8, 128), I32)
        for j in range(4):
            value = counts[dim, j]
            total = total + value
            before = before + jnp.where(j < at, value, 0)
        return before, total

    half_c = pl.ds(pl.multiple_of(512 * c, 512), 512)
    sends = []

    def send_edges(m):
        for q, (buffer, where) in enumerate(
            ((send_r, {"seq": right, "ch": 0}), (send_rr, {"seq": left, "ch": 1}))
        ):
            copy = remote(buffer.at[m], edge.at[m, :, half_c], esend.at[m, q], erecv.at[m, c], where)
            copy.start()
            sends.append(copy)

    for copy in load_res:
        copy.wait()
    for i in groups[0]:
        weight_local(i).start()
    pl.semaphore_wait(barrier, len(greeted))
    sends += count_round(0, jnp.full((8, 128), cnt, I32))
    send_r[0] = picked(cnt - 1, -1)
    send_rr[0] = picked(jnp.int32(0), 1)
    send_edges(0)
    before, total = count_sums(0)
    sends += count_round(1, total)
    for i in groups[0]:
        sends.append(weight_remote(i))
        sends[-1].start()
    send_r[1] = picked(cnt - 1 - T, -1)
    send_rr[1] = picked(jnp.int32(T), 1)
    send_edges(1)
    more, total = count_sums(1)
    before = before + more
    sends += count_round(2, total)
    for g in (1, 2):
        for i in groups[g]:
            weight_local(i).start()
    more, total = count_sums(2)
    place[...] = before + more - SHARD * s
    offset = place[0, 0]
    gap = jnp.where(c == 0, SHARD // 2 - offset, offset + cnt - SHARD)

    def window(core, n):
        sign = 2 * core - 1
        first = jnp.where(core == 1, 1440, 1631) + sign * T * n - offset
        return picked(first, sign)

    def to_peer(h):
        rows = pl.ds(PAD + EDGE * h, EDGE)
        return remote(shift.at[h], x.at[rows, half_c], hsend.at[h], hrecv.at[h], peer)

    for h in (0, 1):

        def shifted(n, _):
            shift[h, pl.ds(pl.multiple_of(T * n, 16), T), :] = window(other, 2 * h + n)
            return 0

        lax.fori_loop(0, 2, shifted, 0)
        sends.append(to_peer(h))
        sends[-1].start()

    def placed(n, _):
        x[pl.ds(pl.multiple_of(PAD + T * n, 16), T), half_c] = window(c, n)
        return 0

    lax.fori_loop(0, 4, placed, 0)
    for i in groups[1]:
        sends.append(weight_remote(i))
        sends[-1].start()

    def block(ref, at, rows, b, dilation, lag, bound, wide_at):
        for n in range(6):
            lanes = pl.ds(256 * n, 256)
            pb[HEAD : HEAD + rows, lanes] = nt(a[:rows, :], w1[b, lanes, :])

        here = HEAD - lag
        for n in range(4):

            def product(k, start):
                return pb[start : start + rows, pl.ds(512 * k + 128 * n, 128)]

            p0, p1, p2 = product(0, here - dilation), product(1, here), product(2, here + dilation)
            if bound is not None:
                t = iota((rows, 128), 0) - jnp.where(last, bound, 1 << 20)
                p0 = jnp.where((t >= 0) & (t < dilation), 0.0, p0)
                p2 = jnp.where((t < 0) & (t >= -dilation), 0.0, p2)
            hid[:rows, pl.ds(128 * n, 128)] = jnp.maximum(p0 + p1 + p2, 0.0).astype(BF)
        if lag:
            carry[b] = pb[rows : rows + HEAD, :]

        for n in range(4):
            lanes = pl.ds(256 * n, 256)
            update = nt(hid[:rows, :], w2[b, lanes, :])
            new = (ref[at : at + rows, lanes].astype(F32) + update).astype(BF)
            ref[at : at + rows, lanes] = new
            if wide_at is not None:
                for q in (0, 1):
                    y32[2 * n + q, wide_at : wide_at + rows, :] = new[:, 128 * q : 128 * (q + 1)].astype(F32)

    def out_tile(i):
        r, q = iota((256, 256), 0), iota((256, 256), 1)
        order = ones_where(jnp.where(c == 0, 255 - r, r) == q)
        same = ones_where(r == q)

        for n in range(4):
            lanes = pl.ds(256 * n, 256)
            rows = nn(order, x[PAD + 96 + 256 * i : PAD + 352 + 256 * i, lanes]).astype(BF)
            ot[i, lanes, :] = nt(same, rows).astype(BF)

    def half(core):
        return pl.ds(pl.multiple_of(512 * core, 512), 512)

    def own_tile(i, start):
        columns = pl.ds(pl.multiple_of(start, 256), 256)
        return (
            pltpu.make_async_copy(ot.at[i, half(c)], out_hbm.at[:, columns], olocal.at[i]),
            remote(ot.at[i, half(other)], out_hbm.at[:, columns], osend.at[i, 0], opeer.at[i], peer),
        )

    def next_tile(i):
        columns = pl.ds(256 * (i - 2), 256)
        return [
            remote(
                ot.at[i, pl.ds(512 * core, 512)],
                out_hbm.at[:, columns],
                osend.at[i, core],
                oleft.at[i - 2],
                {"seq": right, "ch": core},
            )
            for core in (0, 1)
        ]

    def emit(i):
        out_tile(i)
        if i < 2:
            for copy in own_tile(i, jnp.where(c == 0, 1280 - 256 * i, 1536 + 256 * i)):
                copy.start()
        else:

            @pl.when(c == 0)
            def _():
                for copy in own_tile(i, 1280 - 256 * i):
                    copy.start()

            @pl.when(c == 1)
            def _():
                for copy in next_tile(i):
                    copy.start()

    for n in range(4):
        at = PAD + T * n
        if n % 2 == 0:
            to_peer(n // 2).wait_recv()
        if n >= 2:
            m = n - 2
            for core in (0, 1):
                remote(
                    send_r.at[m], edge.at[m, :, pl.ds(512 * core, 512)], esend.at[m, 0], erecv.at[m, core],
                    {"seq": right, "ch": 0},
                ).wait_recv()
            picks = [
                ones_where(T * e + iota((T, T), 1) == T * m + iota((T, T), 0) - gap) for e in range(m + 1)
            ]

            for q in range(4):
                lanes = pl.ds(256 * q, 256)
                total = x[at : at + T, lanes].astype(F32)
                for e in range(m + 1):
                    total = total + nn(picks[e], edge[e, :, lanes])
                x[at : at + T, lanes] = total.astype(BF)
        for b, dilation in ((0, 1), (1, 3)):
            if n == 0:
                need(block_weights(b))
            start = at - 16 * b
            a[...] = jnp.maximum(x[start : start + T, :], jnp.zeros((), BF))
            pb[0:HEAD, :] = carry[b]
            bound = EDGE - (T * n - 16 * b - 16) if n == 2 else None
            block(x, start - 16, T, b, dilation, 16, bound, T * n if b == 1 else None)
        if n == 0:
            for i in groups[2]:
                sends.append(weight_remote(i))
                sends[-1].start()
        for i in ((), (0,), (1, 2), (3,))[n]:
            emit(i)

    def fold(rows):
        def one(n, _):
            for k in range(4):
                lanes = pl.ds(pl.multiple_of(1024 * k + 128 * n, 128), 128)
                z[:rows, lanes] = y32[n, pl.ds(k, rows, stride=4), :].astype(BF)
            return 0

        lax.fori_loop(0, 8, one, 0)

    fold(T)
    need(down_weights(0))

    def down(l, rows, to):
        for n in range(4):
            lanes = pl.ds(256 * n, 256)
            to[:, lanes] = nt(z[:rows, :], dn[l, lanes, :]).astype(BF)

    down(0, T, u)
    for b, dilation in ((2, 1), (3, 3)):
        need(block_weights(b))
        a[...] = jnp.maximum(u[...], jnp.zeros((), BF))
        block(u, 0, T, b, dilation, 0, 160, 0 if b == 3 else None)

    fold(T2)
    need(down_weights(1))
    down(1, T2, v)
    need(block_weights(4))
    a[:T2, :] = jnp.maximum(v[...], jnp.zeros((), BF))
    block(v, 0, T2, 4, 3, 0, 40, None)

    need([28])
    load_cb.wait()
    pj[EMB : 2 * EMB, :] = pj[0:EMB, :]
    pj[2 * EMB : 3 * EMB, :] = pj[0:EMB, :]
    book = cb[...]
    book_hi = book.astype(BF)
    cbk[0:EMB, :] = book_hi
    cbk[EMB : 2 * EMB, :] = book_hi
    cbk[2 * EMB : 3 * EMB, :] = (book - book_hi.astype(F32)).astype(BF)
    book_sq = jnp.sum(book * book, axis=0, keepdims=True)
    frame, row = iota((128, T2), 0), iota((128, T2), 1)
    spot = jnp.where(c == 0, 103 - row, lax.rem(88 + row, 128))
    coarse = nn(ones_where((spot == frame) & (row >= 8) & (row < 72)), v[...]).astype(BF)
    latent = nt(pj[0:EMB, :], coarse)
    thrice = nt(coarse, pj[...])
    hi = thrice.astype(BF)
    lo = (thrice - hi.astype(F32)).astype(BF)
    lane = iota((128, 3 * EMB), 1)
    lhs = jnp.where((lane >= EMB) & (lane < 2 * EMB), lo, hi)
    nearest = jnp.full((128, 1), jnp.inf, F32)
    for q in range(4):
        columns = slice(512 * q, 512 * (q + 1))
        distance = book_sq[:, columns] - 2.0 * nn(lhs, cbk[:, columns])
        nearest = jnp.minimum(nearest, jnp.min(distance, axis=1, keepdims=True))
    diagonal = iota((128, 128), 0) == iota((128, 128), 1)
    nearest = jnp.sum(jnp.where(diagonal, nearest, 0.0), axis=0, keepdims=True)
    nearest = (nearest + jnp.sum(latent * latent, axis=0, keepdims=True)) * (1.0 / EMB)
    msg[0:EMB, :] = latent
    msg[EMB : EMB + 8, :] = jnp.broadcast_to(nearest, (8, 128))
    tell_peer = remote(msg, msg_peer, msend.at[0], mrecv.at[0], peer)
    tell_next = [
        remote(msg, msg_left, msend.at[1 + core], mrecv.at[1], {"seq": right, "ch": core}) for core in (0, 1)
    ]
    tell_peer.start()

    @pl.when(c == 1)
    def _():
        for copy in tell_next:
            copy.start()

    tell_peer.wait_recv()
    tell_next[0].wait_recv()
    lane = iota((EMB + 8, 128), 1)
    own = jnp.where(c == 0, msg[...], msg_peer[...])
    late = jnp.where(c == 0, msg_peer[...], msg[...])
    whole = jnp.where(lane < 32, msg_left[...], jnp.where(lane < 96, own, late))
    lat_ref[...] = whole[0:EMB, :]
    near_ref[...] = whole[EMB : EMB + 8, :]

    tell_peer.wait_send()
    for copy in sends:
        copy.wait_send()
    for i in (0, 1):
        mine, theirs = own_tile(i, jnp.where(c == 0, 1280 - 256 * i, 1536 + 256 * i))
        mine.wait()
        theirs.wait()
        next_tile(2 + i)[0].wait_recv()

    @pl.when(c == 0)
    def _():
        for i in (2, 3):
            mine, theirs = own_tile(i, 1280 - 256 * i)
            mine.wait()
            theirs.wait_send()

    @pl.when(c == 1)
    def _():
        for copy in tell_next:
            copy.wait_send()
        for i in (2, 3):
            own_tile(i, 1280 - 256 * i)[1].wait_recv()
            for copy in next_tile(i):
                copy.wait_send()


def hand_over(sharpest, latent, nearest, sharpest_out, latent_out, nearest_out, sem):
    copies = [
        pltpu.make_async_copy(sharpest.at[pl.ds(64 * i, 64)], sharpest_out.at[pl.ds(64 * i, 64)], sem.at[i])
        for i in range(8)
    ]
    for copy in copies:
        copy.start()
    latent_out[...] = latent[...]
    nearest_out[...] = nearest[0]
    for copy in copies:
        copy.wait()


def on_device(samples, sample_counts, spaced, restore, shrinking, projector, dictionary):
    hbm = pl.BlockSpec(memory_space=pltpu.HBM)
    vmem = pl.BlockSpec(memory_space=pltpu.VMEM)
    dma = pltpu.SemaphoreType.DMA
    sharpest, latent, nearest = pl.pallas_call(
        kernel,
        out_shape=(
            jax.ShapeDtypeStruct((H, SHARD), BF),
            jax.ShapeDtypeStruct((EMB, 128), F32),
            jax.ShapeDtypeStruct((8, 128), F32),
        ),
        in_specs=[pl.BlockSpec(memory_space=pltpu.SMEM)] + [hbm] * 6,
        out_specs=(hbm, vmem, vmem),
        scratch_shapes=[
            pltpu.VMEM((CAP // 128, H, 128), BF),
            pltpu.VMEM((5, 3 * H, C), BF),
            pltpu.VMEM((5, C, H), BF),
            pltpu.VMEM((2, C, 4 * C), BF),
            pltpu.VMEM((3 * EMB, C), BF),
            pltpu.VMEM((EMB, BINS), F32),
            pltpu.VMEM((3 * EMB, BINS), BF),
            pltpu.VMEM((3, 4, 8, 128), I32),
            pltpu.VMEM((8, 128), I32),
            pltpu.VMEM((2, T, C), BF),
            pltpu.VMEM((2, T, H), BF),
            pltpu.VMEM((2, T, H), BF),
            pltpu.VMEM((2, EDGE, H), BF),
            pltpu.VMEM((PAD + 4 * T, C), BF),
            pltpu.VMEM((T, C), BF),
            pltpu.VMEM((HEAD + T + 8, 3 * H), F32),
            pltpu.VMEM((2, HEAD, 3 * H), F32),
            pltpu.VMEM((T, H), BF),
            pltpu.VMEM((8, 4 * T, 128), F32),
            pltpu.VMEM((T, 4 * C), BF),
            pltpu.VMEM((T, C), BF),
            pltpu.VMEM((T2, C), BF),
            pltpu.VMEM((4, C, 256), BF),
            pltpu.VMEM((EMB + 8, 128), F32),
            pltpu.VMEM((EMB + 8, 128), F32),
            pltpu.VMEM((EMB + 8, 128), F32),
            dma((31,)),
            dma((CAP // 128,)),
            dma((29,)),
            dma((29,)),
            dma((3, 3)),
            dma((3, 4)),
            dma((2, 2)),
            dma((2, 2)),
            dma((2,)),
            dma((2,)),
            dma((4,)),
            dma((4, 2)),
            dma((4,)),
            dma((2,)),
            dma((3,)),
            dma((2,)),
        ],
        compiler_params=pltpu.CompilerParams(
            collective_id=0, has_side_effects=True, vmem_limit_bytes=63 * 2**20
        ),
        name="encoder",
    )(sample_counts, samples, spaced, restore, shrinking, projector, dictionary)
    return pl.pallas_call(
        hand_over,
        out_shape=(
            jax.ShapeDtypeStruct((H, SHARD), BF),
            jax.ShapeDtypeStruct((EMB, 128), F32),
            jax.ShapeDtypeStruct((128,), F32),
        ),
        in_specs=[hbm, vmem, vmem],
        out_specs=(hbm, vmem, vmem),
        scratch_shapes=[dma((8,))],
        name="hand_over",
    )(sharpest, latent, nearest)


def solution(mesh):
    return jax.shard_map(
        on_device,
        mesh=mesh,
        in_specs=(
            P("ch", "seq"),
            P("seq"),
            P(None, None, "ch", None),
            P(None, None, "ch"),
            P(None, None, "ch", None),
            P(None, "ch"),
            P(),
        ),
        out_specs=(P("ch", "seq"), P(None, "seq"), P("seq")),
        check_vma=False,
    )
```

```python
import jax
import jax.numpy as jnp
from jax import lax
from jax.experimental import pallas as pl
from jax.experimental.pallas import tpu as pltpu
from jax.sharding import PartitionSpec as P

MESH = pl.DeviceIdType.MESH
BF, F32, I32 = jnp.bfloat16, jnp.float32, jnp.int32
C, H, EMB, BINS, SHARD, CAP = 1024, 512, 64, 2048, 2048, 3072
T = 304
T2 = 80
HEAD = 24
PAD = 32
EDGE = 2 * T


def nt(a, b):
    return lax.dot_general(a, b, (((1,), (1,)), ((), ())), preferred_element_type=F32)


def nn(a, b):
    return jnp.dot(a, b, preferred_element_type=F32)


def iota(shape, dim):
    return lax.broadcasted_iota(I32, shape, dim)


def ones_where(mask):
    return jnp.where(mask, 1.0, 0.0).astype(BF)


def kernel(
    cnt_ref, res_hbm, w1_hbm, w2_hbm, dn_hbm, pj_hbm, cb_hbm,
    out_hbm, lat_ref, near_ref,
    res, w1, w2, dn, pj, cb, cbk, counts, place, edge, send_r, send_rr, shift, x, a, pb, carry, hid, y32, z, u, v, ot,
    msg, msg_peer, msg_left,
    lsem, rsem, wsend, wrecv, csend, crecv, esend, erecv, hsend, hrecv, olocal, osend, opeer, oleft, msend, mrecv,
):
    s, c = lax.axis_index("seq"), lax.axis_index("ch")
    n_seq = lax.axis_size("seq")
    right, left = lax.rem(s + 1, n_seq), lax.rem(s + n_seq - 1, n_seq)
    other = 1 - c
    peer = {"seq": s, "ch": other}
    rounds = ((lax.rem(s, 4), 1), (lax.rem(s // 4, 4), 4), (s // 16, 16))
    last = (s == n_seq - 1) & (c == 1)

    def remote(src, dst, send, recv, where):
        return pltpu.make_async_remote_copy(
            src_ref=src, dst_ref=dst, send_sem=send, recv_sem=recv, device_id=where, device_id_type=MESH
        )

    def weight(i, on):
        if i < 15:
            b, k = divmod(i, 3)
            tap = k + (1 - on) * (2 - 2 * k)
            return w1_hbm.at[b, k], w1.at[b, pl.ds(pl.multiple_of(512 * tap + 256 * c, 256), 256)]
        if i < 20:
            return w2_hbm.at[i - 15], w2.at[i - 15, :, pl.ds(pl.multiple_of(256 * c, 256), 256)]
        if i < 28:
            l, k = divmod(i - 20, 4)
            tap = k + (1 - on) * (3 - 2 * k)
            return dn_hbm.at[l, k], dn.at[
                l, pl.ds(pl.multiple_of(512 * c, 512), 512), pl.ds(pl.multiple_of(1024 * tap, 1024), 1024)
            ]
        return pj_hbm, pj.at[pl.ds(0, EMB), pl.ds(pl.multiple_of(512 * c, 512), 512)]

    def weight_local(i):
        return pltpu.make_async_copy(*weight(i, c), lsem.at[i])

    def weight_remote(i):
        return remote(*weight(i, other), wsend.at[i], wrecv.at[i], peer)

    def block_weights(b):
        return [3 * b, 3 * b + 1, 3 * b + 2, 15 + b]

    def down_weights(l):
        return [20 + 4 * l + k for k in range(4)]

    def need(items):
        for i in items:
            weight_local(i).wait()
            weight_remote(i).wait_recv()

    groups = [
        block_weights(0) + block_weights(1),
        down_weights(0) + block_weights(2),
        block_weights(3) + down_weights(1) + block_weights(4) + [28],
    ]
    load_res = [
        pltpu.make_async_copy(res_hbm.at[:, pl.ds(128 * k, 128)], res.at[k], rsem.at[k]) for k in range(CAP // 128)
    ]
    load_cb = pltpu.make_async_copy(cb_hbm, cb, lsem.at[30])
    for copy in load_res:
        copy.start()
    load_cb.start()

    barrier = pltpu.get_barrier_semaphore()
    greeted = [peer] + [{"seq": chip, "ch": core} for chip in (left, right) for core in (0, 1)]
    partners = [[], [], []]
    for dim, (at, stride) in enumerate(rounds):
        for q in (1, 2, 3):
            j = lax.rem(at + q, 4)
            partners[dim].append((j, {"seq": s + (j - at) * stride, "ch": c}))
            greeted.append(partners[dim][-1][1])
    for where in greeted:
        pl.semaphore_signal(barrier, inc=1, device_id=where, device_id_type=MESH)

    cnt = cnt_ref[0]
    x[0:PAD, :] = jnp.zeros((PAD, C), BF)
    pb[...] = jnp.zeros(pb.shape, F32)
    carry[...] = jnp.zeros(carry.shape, F32)

    def picked(first, sign):
        lowest = jnp.maximum(jnp.minimum(first, first + sign * (T - 1)), 0)
        tile = jnp.minimum(lax.shift_right_logical(lowest, 7), CAP // 128 - 4)
        column = 128 * tile + iota((T, 512), 1)
        pick = ones_where((column == first + sign * iota((T, 512), 0)) & (column < cnt))
        found = jnp.concatenate([res[tile + q] for q in range(4)], axis=1)
        return nt(pick, found).astype(BF)

    def count_round(dim, value):
        at = rounds[dim][0]
        counts[dim, at] = value
        copies = []
        for q, (j, where) in enumerate(partners[dim]):
            copies.append(
                remote(counts.at[dim, at], counts.at[dim, at], csend.at[dim, q], crecv.at[dim, at], where)
            )
            copies[-1].start()
        return copies

    def count_sums(dim):
        at = rounds[dim][0]
        for q, (j, where) in enumerate(partners[dim]):
            remote(counts.at[dim, j], counts.at[dim, j], csend.at[dim, q], crecv.at[dim, j], where).wait_recv()
        before, total = jnp.zeros((8, 128), I32), jnp.zeros((8, 128), I32)
        for j in range(4):
            value = counts[dim, j]
            total = total + value
            before = before + jnp.where(j < at, value, 0)
        return before, total

    half_c = pl.ds(pl.multiple_of(512 * c, 512), 512)
    sends = []

    def send_edges(m):
        for q, (buffer, where) in enumerate(
            ((send_r, {"seq": right, "ch": 0}), (send_rr, {"seq": left, "ch": 1}))
        ):
            copy = remote(buffer.at[m], edge.at[m, :, half_c], esend.at[m, q], erecv.at[m, c], where)
            copy.start()
            sends.append(copy)

    for copy in load_res:
        copy.wait()
    for i in groups[0]:
        weight_local(i).start()
    pl.semaphore_wait(barrier, len(greeted))
    sends += count_round(0, jnp.full((8, 128), cnt, I32))
    send_r[0] = picked(cnt - 1, -1)
    send_rr[0] = picked(jnp.int32(0), 1)
    send_edges(0)
    before, total = count_sums(0)
    sends += count_round(1, total)
    for i in groups[0]:
        sends.append(weight_remote(i))
        sends[-1].start()
    send_r[1] = picked(cnt - 1 - T, -1)
    send_rr[1] = picked(jnp.int32(T), 1)
    send_edges(1)
    more, total = count_sums(1)
    before = before + more
    sends += count_round(2, total)
    for g in (1, 2):
        for i in groups[g]:
            weight_local(i).start()
    more, total = count_sums(2)
    place[...] = before + more - SHARD * s
    offset = place[0, 0]
    gap = jnp.where(c == 0, SHARD // 2 - offset, offset + cnt - SHARD)

    def window(core, n):
        sign = 2 * core - 1
        first = jnp.where(core == 1, 1440, 1631) + sign * T * n - offset
        return picked(first, sign)

    def to_peer(h):
        rows = pl.ds(PAD + EDGE * h, EDGE)
        return remote(shift.at[h], x.at[rows, half_c], hsend.at[h], hrecv.at[h], peer)

    for h in (0, 1):

        def shifted(n, _):
            shift[h, pl.ds(pl.multiple_of(T * n, 16), T), :] = window(other, 2 * h + n)
            return 0

        lax.fori_loop(0, 2, shifted, 0)
        sends.append(to_peer(h))
        sends[-1].start()

    def placed(n, _):
        x[pl.ds(pl.multiple_of(PAD + T * n, 16), T), half_c] = window(c, n)
        return 0

    lax.fori_loop(0, 4, placed, 0)
    for i in groups[1]:
        sends.append(weight_remote(i))
        sends[-1].start()

    def block(ref, at, rows, b, dilation, lag, bound, wide_at):
        for n in range(6):
            lanes = pl.ds(256 * n, 256)
            pb[HEAD : HEAD + rows, lanes] = nt(a[:rows, :], w1[b, lanes, :])

        here = HEAD - lag
        for n in range(4):

            def product(k, start):
                return pb[start : start + rows, pl.ds(512 * k + 128 * n, 128)]

            p0, p1, p2 = product(0, here - dilation), product(1, here), product(2, here + dilation)
            if bound is not None:
                t = iota((rows, 128), 0) - jnp.where(last, bound, 1 << 20)
                p0 = jnp.where((t >= 0) & (t < dilation), 0.0, p0)
                p2 = jnp.where((t < 0) & (t >= -dilation), 0.0, p2)
            hid[:rows, pl.ds(128 * n, 128)] = jnp.maximum(p0 + p1 + p2, 0.0).astype(BF)
        if lag:
            carry[b] = pb[rows : rows + HEAD, :]

        for n in range(4):
            lanes = pl.ds(256 * n, 256)
            update = nt(hid[:rows, :], w2[b, lanes, :])
            new = (ref[at : at + rows, lanes].astype(F32) + update).astype(BF)
            ref[at : at + rows, lanes] = new
            if wide_at is not None:
                for q in (0, 1):
                    y32[2 * n + q, wide_at : wide_at + rows, :] = new[:, 128 * q : 128 * (q + 1)].astype(F32)

    def out_tile(i):
        r, q = iota((256, 256), 0), iota((256, 256), 1)
        order = ones_where(jnp.where(c == 0, 255 - r, r) == q)
        same = ones_where(r == q)

        for n in range(4):
            lanes = pl.ds(256 * n, 256)
            rows = nn(order, x[PAD + 96 + 256 * i : PAD + 352 + 256 * i, lanes]).astype(BF)
            ot[i, lanes, :] = nt(same, rows).astype(BF)

    def half(core):
        return pl.ds(pl.multiple_of(512 * core, 512), 512)

    def own_tile(i, start):
        columns = pl.ds(pl.multiple_of(start, 256), 256)
        return (
            pltpu.make_async_copy(ot.at[i, half(c)], out_hbm.at[:, columns], olocal.at[i]),
            remote(ot.at[i, half(other)], out_hbm.at[:, columns], osend.at[i, 0], opeer.at[i], peer),
        )

    def next_tile(i):
        columns = pl.ds(256 * (i - 2), 256)
        return [
            remote(
                ot.at[i, pl.ds(512 * core, 512)],
                out_hbm.at[:, columns],
                osend.at[i, core],
                oleft.at[i - 2],
                {"seq": right, "ch": core},
            )
            for core in (0, 1)
        ]

    def emit(i):
        out_tile(i)
        if i < 2:
            for copy in own_tile(i, jnp.where(c == 0, 1280 - 256 * i, 1536 + 256 * i)):
                copy.start()
        else:

            @pl.when(c == 0)
            def _():
                for copy in own_tile(i, 1280 - 256 * i):
                    copy.start()

            @pl.when(c == 1)
            def _():
                for copy in next_tile(i):
                    copy.start()

    for n in range(4):
        at = PAD + T * n
        if n % 2 == 0:
            to_peer(n // 2).wait_recv()
        if n >= 2:
            m = n - 2
            for core in (0, 1):
                remote(
                    send_r.at[m], edge.at[m, :, pl.ds(512 * core, 512)], esend.at[m, 0], erecv.at[m, core],
                    {"seq": right, "ch": 0},
                ).wait_recv()
            picks = [
                ones_where(T * e + iota((T, T), 1) == T * m + iota((T, T), 0) - gap) for e in range(m + 1)
            ]

            for q in range(4):
                lanes = pl.ds(256 * q, 256)
                total = x[at : at + T, lanes].astype(F32)
                for e in range(m + 1):
                    total = total + nn(picks[e], edge[e, :, lanes])
                x[at : at + T, lanes] = total.astype(BF)
        for b, dilation in ((0, 1), (1, 3)):
            if n == 0:
                need(block_weights(b))
            start = at - 16 * b
            a[...] = jnp.maximum(x[start : start + T, :], jnp.zeros((), BF))
            pb[0:HEAD, :] = carry[b]
            bound = EDGE - (T * n - 16 * b - 16) if n == 2 else None
            block(x, start - 16, T, b, dilation, 16, bound, T * n if b == 1 else None)
        if n == 0:
            for i in groups[2]:
                sends.append(weight_remote(i))
                sends[-1].start()
        for i in ((), (0,), (1, 2), (3,))[n]:
            emit(i)

    def fold(rows):
        def one(n, _):
            for k in range(4):
                lanes = pl.ds(pl.multiple_of(1024 * k + 128 * n, 128), 128)
                z[:rows, lanes] = y32[n, pl.ds(k, rows, stride=4), :].astype(BF)
            return 0

        lax.fori_loop(0, 8, one, 0)

    fold(T)
    need(down_weights(0))

    def down(l, rows, to):
        for n in range(4):
            lanes = pl.ds(256 * n, 256)
            to[:, lanes] = nt(z[:rows, :], dn[l, lanes, :]).astype(BF)

    down(0, T, u)
    for b, dilation in ((2, 1), (3, 3)):
        need(block_weights(b))
        a[...] = jnp.maximum(u[...], jnp.zeros((), BF))
        block(u, 0, T, b, dilation, 0, 160, 0 if b == 3 else None)

    fold(T2)
    need(down_weights(1))
    down(1, T2, v)
    need(block_weights(4))
    a[:T2, :] = jnp.maximum(v[...], jnp.zeros((), BF))
    block(v, 0, T2, 4, 3, 0, 40, None)

    need([28])
    load_cb.wait()
    pj[EMB : 2 * EMB, :] = pj[0:EMB, :]
    pj[2 * EMB : 3 * EMB, :] = pj[0:EMB, :]
    book = cb[...]
    book_hi = book.astype(BF)
    cbk[0:EMB, :] = book_hi
    cbk[EMB : 2 * EMB, :] = book_hi
    cbk[2 * EMB : 3 * EMB, :] = (book - book_hi.astype(F32)).astype(BF)
    book_sq = jnp.sum(book * book, axis=0, keepdims=True)
    frame, row = iota((128, T2), 0), iota((128, T2), 1)
    spot = jnp.where(c == 0, 103 - row, lax.rem(88 + row, 128))
    coarse = nn(ones_where((spot == frame) & (row >= 8) & (row < 72)), v[...]).astype(BF)
    latent = nt(pj[0:EMB, :], coarse)
    thrice = nt(coarse, pj[...])
    hi = thrice.astype(BF)
    lo = (thrice - hi.astype(F32)).astype(BF)
    lane = iota((128, 3 * EMB), 1)
    lhs = jnp.where((lane >= EMB) & (lane < 2 * EMB), lo, hi)
    nearest = jnp.full((128, 1), jnp.inf, F32)
    for q in range(4):
        columns = slice(512 * q, 512 * (q + 1))
        distance = book_sq[:, columns] - 2.0 * nn(lhs, cbk[:, columns])
        nearest = jnp.minimum(nearest, jnp.min(distance, axis=1, keepdims=True))
    diagonal = iota((128, 128), 0) == iota((128, 128), 1)
    nearest = jnp.sum(jnp.where(diagonal, nearest, 0.0), axis=0, keepdims=True)
    nearest = (nearest + jnp.sum(latent * latent, axis=0, keepdims=True)) * (1.0 / EMB)
    msg[0:EMB, :] = latent
    msg[EMB : EMB + 8, :] = jnp.broadcast_to(nearest, (8, 128))
    tell_peer = remote(msg, msg_peer, msend.at[0], mrecv.at[0], peer)
    tell_next = [
        remote(msg, msg_left, msend.at[1 + core], mrecv.at[1], {"seq": right, "ch": core}) for core in (0, 1)
    ]
    tell_peer.start()

    @pl.when(c == 1)
    def _():
        for copy in tell_next:
            copy.start()

    tell_peer.wait_recv()
    tell_next[0].wait_recv()
    lane = iota((EMB + 8, 128), 1)
    own = jnp.where(c == 0, msg[...], msg_peer[...])
    late = jnp.where(c == 0, msg_peer[...], msg[...])
    whole = jnp.where(lane < 32, msg_left[...], jnp.where(lane < 96, own, late))
    lat_ref[...] = whole[0:EMB, :]
    near_ref[...] = whole[EMB : EMB + 8, :]

    tell_peer.wait_send()
    for copy in sends:
        copy.wait_send()
    for i in (0, 1):
        mine, theirs = own_tile(i, jnp.where(c == 0, 1280 - 256 * i, 1536 + 256 * i))
        mine.wait()
        theirs.wait()
        next_tile(2 + i)[0].wait_recv()

    @pl.when(c == 0)
    def _():
        for i in (2, 3):
            mine, theirs = own_tile(i, 1280 - 256 * i)
            mine.wait()
            theirs.wait_send()

    @pl.when(c == 1)
    def _():
        for copy in tell_next:
            copy.wait_send()
        for i in (2, 3):
            own_tile(i, 1280 - 256 * i)[1].wait_recv()
            for copy in next_tile(i):
                copy.wait_send()


def hand_over(sharpest, latent, nearest, sharpest_out, latent_out, nearest_out, held, sem):
    parts = [pl.ds(64 * i, 64) for i in range(8)]
    reads = [pltpu.make_async_copy(sharpest.at[p], held.at[p], sem.at[0, i]) for i, p in enumerate(parts)]
    writes = [pltpu.make_async_copy(held.at[p], sharpest_out.at[p], sem.at[1, i]) for i, p in enumerate(parts)]
    for copy in reads:
        copy.start()
    latent_out[...] = latent[...]
    nearest_out[...] = nearest[0]
    for read, write in zip(reads, writes):
        read.wait()
        write.start()
    for copy in writes:
        copy.wait()


def on_device(samples, sample_counts, spaced, restore, shrinking, projector, dictionary):
    hbm = pl.BlockSpec(memory_space=pltpu.HBM)
    vmem = pl.BlockSpec(memory_space=pltpu.VMEM)
    dma = pltpu.SemaphoreType.DMA
    sharpest, latent, nearest = pl.pallas_call(
        kernel,
        out_shape=(
            jax.ShapeDtypeStruct((H, SHARD), BF),
            jax.ShapeDtypeStruct((EMB, 128), F32),
            jax.ShapeDtypeStruct((8, 128), F32),
        ),
        in_specs=[pl.BlockSpec(memory_space=pltpu.SMEM)] + [hbm] * 6,
        out_specs=(hbm, vmem, vmem),
        scratch_shapes=[
            pltpu.VMEM((CAP // 128, H, 128), BF),
            pltpu.VMEM((5, 3 * H, C), BF),
            pltpu.VMEM((5, C, H), BF),
            pltpu.VMEM((2, C, 4 * C), BF),
            pltpu.VMEM((3 * EMB, C), BF),
            pltpu.VMEM((EMB, BINS), F32),
            pltpu.VMEM((3 * EMB, BINS), BF),
            pltpu.VMEM((3, 4, 8, 128), I32),
            pltpu.VMEM((8, 128), I32),
            pltpu.VMEM((2, T, C), BF),
            pltpu.VMEM((2, T, H), BF),
            pltpu.VMEM((2, T, H), BF),
            pltpu.VMEM((2, EDGE, H), BF),
            pltpu.VMEM((PAD + 4 * T, C), BF),
            pltpu.VMEM((T, C), BF),
            pltpu.VMEM((HEAD + T + 8, 3 * H), F32),
            pltpu.VMEM((2, HEAD, 3 * H), F32),
            pltpu.VMEM((T, H), BF),
            pltpu.VMEM((8, 4 * T, 128), F32),
            pltpu.VMEM((T, 4 * C), BF),
            pltpu.VMEM((T, C), BF),
            pltpu.VMEM((T2, C), BF),
            pltpu.VMEM((4, C, 256), BF),
            pltpu.VMEM((EMB + 8, 128), F32),
            pltpu.VMEM((EMB + 8, 128), F32),
            pltpu.VMEM((EMB + 8, 128), F32),
            dma((31,)),
            dma((CAP // 128,)),
            dma((29,)),
            dma((29,)),
            dma((3, 3)),
            dma((3, 4)),
            dma((2, 2)),
            dma((2, 2)),
            dma((2,)),
            dma((2,)),
            dma((4,)),
            dma((4, 2)),
            dma((4,)),
            dma((2,)),
            dma((3,)),
            dma((2,)),
        ],
        compiler_params=pltpu.CompilerParams(
            collective_id=0, has_side_effects=True, vmem_limit_bytes=63 * 2**20
        ),
        name="encoder",
    )(sample_counts, samples, spaced, restore, shrinking, projector, dictionary)
    return pl.pallas_call(
        hand_over,
        out_shape=(
            jax.ShapeDtypeStruct((H, SHARD), BF),
            jax.ShapeDtypeStruct((EMB, 128), F32),
            jax.ShapeDtypeStruct((128,), F32),
        ),
        in_specs=[hbm, vmem, vmem],
        out_specs=(hbm, vmem, vmem),
        scratch_shapes=[pltpu.VMEM((H, SHARD), BF), dma((2, 8))],
        name="hand_over",
    )(sharpest, latent, nearest)


def solution(mesh):
    return jax.shard_map(
        on_device,
        mesh=mesh,
        in_specs=(
            P("ch", "seq"),
            P("seq"),
            P(None, None, "ch", None),
            P(None, None, "ch"),
            P(None, None, "ch", None),
            P(None, "ch"),
            P(),
        ),
        out_specs=(P("ch", "seq"), P(None, "seq"), P("seq")),
        check_vma=False,
    )
```

```python
import jax
import jax.numpy as jnp
from jax import lax
from jax.experimental import pallas as pl
from jax.experimental.pallas import tpu as pltpu
from jax.sharding import PartitionSpec as P

MESH = pl.DeviceIdType.MESH
BF, F32, I32 = jnp.bfloat16, jnp.float32, jnp.int32
C, H, EMB, BINS, SHARD, CAP = 1024, 512, 64, 2048, 2048, 3072
T = 304
T2 = 80
N_SEQ = 64
HEAD = 24
PAD = 32
EDGE = 2 * T


def nt(a, b):
    return lax.dot_general(a, b, (((1,), (1,)), ((), ())), preferred_element_type=F32)


def nn(a, b):
    return jnp.dot(a, b, preferred_element_type=F32)


def iota(shape, dim):
    return lax.broadcasted_iota(I32, shape, dim)


def ones_where(mask):
    return jnp.where(mask, 1.0, 0.0).astype(BF)


def kernel(
    cnt_ref, res_hbm, w1_hbm, w2_hbm, dn_hbm, pj_hbm, cb_hbm,
    out_hbm, lat_ref, near_ref,
    res, w1, w2, dn, pj, cb, cbk, counts, place, edge, send_r, send_rr, shift, x, a, pb, carry, hid, y32, z, u, v,
    msg, msg_peer, msg_left,
    lsem, rsem, wsend, wrecv, csend, crecv, esend, erecv, hsend, hrecv, olocal, osend, opeer, oleft, msend, mrecv,
):
    s, c = lax.axis_index("seq"), lax.axis_index("ch")
    n_seq = lax.axis_size("seq")
    right, left = lax.rem(s + 1, n_seq), lax.rem(s + n_seq - 1, n_seq)
    other = 1 - c
    peer = {"seq": s, "ch": other}
    last = (s == n_seq - 1) & (c == 1)

    def remote(src, dst, send, recv, where):
        return pltpu.make_async_remote_copy(
            src_ref=src, dst_ref=dst, send_sem=send, recv_sem=recv, device_id=where, device_id_type=MESH
        )

    def weight(i, on):
        if i < 15:
            b, k = divmod(i, 3)
            tap = k + (1 - on) * (2 - 2 * k)
            return w1_hbm.at[b, k], w1.at[b, pl.ds(pl.multiple_of(512 * tap + 256 * c, 256), 256)]
        if i < 20:
            return w2_hbm.at[i - 15], w2.at[i - 15, :, pl.ds(pl.multiple_of(256 * c, 256), 256)]
        if i < 28:
            l, k = divmod(i - 20, 4)
            tap = k + (1 - on) * (3 - 2 * k)
            return dn_hbm.at[l, k], dn.at[
                l, pl.ds(pl.multiple_of(512 * c, 512), 512), pl.ds(pl.multiple_of(1024 * tap, 1024), 1024)
            ]
        return pj_hbm, pj.at[pl.ds(0, EMB), pl.ds(pl.multiple_of(512 * c, 512), 512)]

    def weight_local(i):
        return pltpu.make_async_copy(*weight(i, c), lsem.at[i])

    def weight_remote(i):
        return remote(*weight(i, other), wsend.at[i], wrecv.at[i], peer)

    def block_weights(b):
        return [3 * b, 3 * b + 1, 3 * b + 2, 15 + b]

    def down_weights(l):
        return [20 + 4 * l + k for k in range(4)]

    def need(items):
        for i in items:
            weight_local(i).wait()
            weight_remote(i).wait_recv()

    groups = [
        block_weights(0) + block_weights(1),
        down_weights(0) + block_weights(2),
        block_weights(3) + down_weights(1) + block_weights(4) + [28],
    ]
    load_res = [
        pltpu.make_async_copy(res_hbm.at[:, pl.ds(128 * k, 128)], res.at[k], rsem.at[k]) for k in range(CAP // 128)
    ]
    load_cb = pltpu.make_async_copy(cb_hbm, cb, lsem.at[30])
    for copy in load_res:
        copy.start()
    load_cb.start()

    barrier = pltpu.get_barrier_semaphore()
    def chip(q):
        return {"seq": lax.rem(s + q, n_seq), "ch": c}

    def greet(q, _):
        pl.semaphore_signal(barrier, inc=1, device_id=chip(q), device_id_type=MESH)
        return 0

    lax.fori_loop(1, N_SEQ, greet, 0)
    for where in (peer, {"seq": left, "ch": other}, {"seq": right, "ch": other}):
        pl.semaphore_signal(barrier, inc=1, device_id=where, device_id_type=MESH)

    cnt = cnt_ref[0]
    x[0:PAD, :] = jnp.zeros((PAD, C), BF)
    pb[...] = jnp.zeros(pb.shape, F32)
    carry[...] = jnp.zeros(carry.shape, F32)

    def picked(first, sign):
        lowest = jnp.maximum(jnp.minimum(first, first + sign * (T - 1)), 0)
        tile = jnp.minimum(lax.shift_right_logical(lowest, 7), CAP // 128 - 4)
        column = 128 * tile + iota((T, 512), 1)
        pick = ones_where((column == first + sign * iota((T, 512), 0)) & (column < cnt))
        found = jnp.concatenate([res[tile + q] for q in range(4)], axis=1)
        return nt(pick, found).astype(BF)

    def tell_count(q, _):
        remote(counts.at[s], counts.at[s], csend.at[0], crecv.at[0], chip(q)).start()
        return 0

    others = pl.ds(0, N_SEQ - 1)
    all_counts = remote(counts.at[others], counts.at[others], csend.at[0], crecv.at[0], chip(1))

    half_c = pl.ds(pl.multiple_of(512 * c, 512), 512)
    sends = []

    def send_edges(m):
        for q, (buffer, where) in enumerate(
            ((send_r, {"seq": right, "ch": 0}), (send_rr, {"seq": left, "ch": 1}))
        ):
            copy = remote(buffer.at[m], edge.at[m, :, half_c], esend.at[m, q], erecv.at[m, c], where)
            copy.start()
            sends.append(copy)

    for copy in load_res:
        copy.wait()
    for i in groups[0]:
        weight_local(i).start()
    pl.semaphore_wait(barrier, N_SEQ + 2)
    counts[s] = jnp.full((8, 128), cnt, I32)
    lax.fori_loop(1, N_SEQ, tell_count, 0)
    send_r[0] = picked(cnt - 1, -1)
    send_rr[0] = picked(jnp.int32(0), 1)
    send_edges(0)
    for i in groups[0]:
        sends.append(weight_remote(i))
        sends[-1].start()
    send_r[1] = picked(cnt - 1 - T, -1)
    send_rr[1] = picked(jnp.int32(T), 1)
    send_edges(1)
    for g in (1, 2):
        for i in groups[g]:
            weight_local(i).start()
    all_counts.wait_recv()
    earlier = iota((N_SEQ, 8, 128), 0) < s
    place[...] = jnp.sum(jnp.where(earlier, counts[...], 0), axis=0) - SHARD * s
    offset = place[0, 0]
    gap = jnp.where(c == 0, SHARD // 2 - offset, offset + cnt - SHARD)

    def window(core, n):
        sign = 2 * core - 1
        first = jnp.where(core == 1, 1440, 1631) + sign * T * n - offset
        return picked(first, sign)

    def to_peer(h):
        rows = pl.ds(PAD + EDGE * h, EDGE)
        return remote(shift.at[h], x.at[rows, half_c], hsend.at[h], hrecv.at[h], peer)

    def place_half(h):
        def shifted(n, _):
            shift[h, pl.ds(pl.multiple_of(T * n, 16), T), :] = window(other, 2 * h + n)
            return 0

        lax.fori_loop(0, 2, shifted, 0)
        sends.append(to_peer(h))
        sends[-1].start()

        def placed(n, _):
            x[pl.ds(pl.multiple_of(PAD + EDGE * h + T * n, 16), T), half_c] = window(c, 2 * h + n)
            return 0

        lax.fori_loop(0, 2, placed, 0)

    place_half(0)
    for i in groups[1]:
        sends.append(weight_remote(i))
        sends[-1].start()

    def block(ref, at, rows, b, dilation, lag, bound, wide_at):
        for n in range(6):
            lanes = pl.ds(256 * n, 256)
            pb[HEAD : HEAD + rows, lanes] = nt(a[:rows, :], w1[b, lanes, :])

        here = HEAD - lag
        for n in range(4):

            def product(k, start):
                return pb[start : start + rows, pl.ds(512 * k + 128 * n, 128)]

            p0, p1, p2 = product(0, here - dilation), product(1, here), product(2, here + dilation)
            if bound is not None:
                t = iota((rows, 128), 0) - jnp.where(last, bound, 1 << 20)
                p0 = jnp.where((t >= 0) & (t < dilation), 0.0, p0)
                p2 = jnp.where((t < 0) & (t >= -dilation), 0.0, p2)
            hid[:rows, pl.ds(128 * n, 128)] = jnp.maximum(p0 + p1 + p2, 0.0).astype(BF)
        if lag:
            carry[b] = pb[rows : rows + HEAD, :]

        for n in range(4):
            lanes = pl.ds(256 * n, 256)
            update = nt(hid[:rows, :], w2[b, lanes, :])
            new = (ref[at : at + rows, lanes].astype(F32) + update).astype(BF)
            ref[at : at + rows, lanes] = new
            if wide_at is not None:
                for q in (0, 1):
                    y32[2 * n + q, wide_at : wide_at + rows, :] = new[:, 128 * q : 128 * (q + 1)].astype(F32)

    def half(core):
        return pl.ds(pl.multiple_of(512 * core, 512), 512)

    def own_rows(i, first, count, start):
        rows, to = pl.ds(PAD + first, count), pl.ds(pl.multiple_of(start, 16), count)
        return (
            lambda: pltpu.make_async_copy(x.at[rows, half(c)], out_hbm.at[to], olocal.at[i]),
            lambda: remote(x.at[rows, half(other)], out_hbm.at[to], osend.at[i, 0], opeer.at[i], peer),
        )

    def next_rows(i, first, count):
        return [
            remote(
                x.at[pl.ds(PAD + first, count), pl.ds(512 * core, 512)],
                out_hbm.at[pl.ds(first - EDGE, count)],
                osend.at[i, core],
                oleft.at[i - 2],
                {"seq": right, "ch": core},
            )
            for core in (0, 1)
        ]

    pieces = ((96, 176), (272, 336), (608, 272), (880, 240))

    def emit(i):
        first, count = pieces[i]
        if i < 2:
            for copy in own_rows(i, first, count, jnp.where(c == 0, 416 + first, 1440 + first)):
                copy().start()
        else:

            @pl.when(c == 0)
            def _():
                for copy in own_rows(i, first, count, 416 + first):
                    copy().start()

            @pl.when(c == 1)
            def _():
                for copy in next_rows(i, first, count):
                    copy.start()

    for n in range(4):
        at = PAD + T * n
        if n % 2 == 0:
            to_peer(n // 2).wait_recv()
        if n >= 2:
            m = n - 2
            for core in (0, 1):
                remote(
                    send_r.at[m], edge.at[m, :, pl.ds(512 * core, 512)], esend.at[m, 0], erecv.at[m, core],
                    {"seq": right, "ch": 0},
                ).wait_recv()
            picks = [
                ones_where(T * e + iota((T, T), 1) == T * m + iota((T, T), 0) - gap) for e in range(m + 1)
            ]

            for q in range(4):
                lanes = pl.ds(256 * q, 256)
                total = x[at : at + T, lanes].astype(F32)
                for e in range(m + 1):
                    total = total + nn(picks[e], edge[e, :, lanes])
                x[at : at + T, lanes] = total.astype(BF)
        if n == 1:
            place_half(1)
        for b, dilation in ((0, 1), (1, 3)):
            if n == 0:
                need(block_weights(b))
            start = at - 16 * b
            a[...] = jnp.maximum(x[start : start + T, :], jnp.zeros((), BF))
            pb[0:HEAD, :] = carry[b]
            bound = EDGE - (T * n - 16 * b - 16) if n == 2 else None
            block(x, start - 16, T, b, dilation, 16, bound, T * n if b == 1 else None)
        if n == 0:
            for i in groups[2]:
                sends.append(weight_remote(i))
                sends[-1].start()
        for i in ((0,), (), (1, 2), (3,))[n]:
            emit(i)

    def fold(rows):
        def one(n, _):
            for k in range(4):
                lanes = pl.ds(pl.multiple_of(1024 * k + 128 * n, 128), 128)
                z[:rows, lanes] = y32[n, pl.ds(k, rows, stride=4), :].astype(BF)
            return 0

        lax.fori_loop(0, 8, one, 0)

    fold(T)
    need(down_weights(0))

    def down(l, rows, to):
        for n in range(4):
            lanes = pl.ds(256 * n, 256)
            to[:, lanes] = nt(z[:rows, :], dn[l, lanes, :]).astype(BF)

    down(0, T, u)
    for b, dilation in ((2, 1), (3, 3)):
        need(block_weights(b))
        a[...] = jnp.maximum(u[...], jnp.zeros((), BF))
        block(u, 0, T, b, dilation, 0, 160, 0 if b == 3 else None)

    fold(T2)
    need(down_weights(1))
    down(1, T2, v)
    need(block_weights(4))
    a[:T2, :] = jnp.maximum(v[...], jnp.zeros((), BF))
    block(v, 0, T2, 4, 3, 0, 40, None)

    need([28])
    load_cb.wait()
    pj[EMB : 2 * EMB, :] = pj[0:EMB, :]
    pj[2 * EMB : 3 * EMB, :] = pj[0:EMB, :]
    book = cb[...]
    book_hi = book.astype(BF)
    cbk[0:EMB, :] = book_hi
    cbk[EMB : 2 * EMB, :] = book_hi
    cbk[2 * EMB : 3 * EMB, :] = (book - book_hi.astype(F32)).astype(BF)
    book_sq = jnp.sum(book * book, axis=0, keepdims=True)
    frame, row = iota((128, T2), 0), iota((128, T2), 1)
    spot = jnp.where(c == 0, 103 - row, lax.rem(88 + row, 128))
    coarse = nn(ones_where((spot == frame) & (row >= 8) & (row < 72)), v[...]).astype(BF)
    latent = nt(pj[0:EMB, :], coarse)
    thrice = nt(coarse, pj[...])
    hi = thrice.astype(BF)
    lo = (thrice - hi.astype(F32)).astype(BF)
    lane = iota((128, 3 * EMB), 1)
    lhs = jnp.where((lane >= EMB) & (lane < 2 * EMB), lo, hi)
    nearest = jnp.full((128, 1), jnp.inf, F32)
    for q in range(4):
        columns = slice(512 * q, 512 * (q + 1))
        distance = book_sq[:, columns] - 2.0 * nn(lhs, cbk[:, columns])
        nearest = jnp.minimum(nearest, jnp.min(distance, axis=1, keepdims=True))
    diagonal = iota((128, 128), 0) == iota((128, 128), 1)
    nearest = jnp.sum(jnp.where(diagonal, nearest, 0.0), axis=0, keepdims=True)
    nearest = (nearest + jnp.sum(latent * latent, axis=0, keepdims=True)) * (1.0 / EMB)
    msg[0:EMB, :] = latent
    msg[EMB : EMB + 8, :] = jnp.broadcast_to(nearest, (8, 128))
    tell_peer = remote(msg, msg_peer, msend.at[0], mrecv.at[0], peer)
    tell_next = [
        remote(msg, msg_left, msend.at[1 + core], mrecv.at[1], {"seq": right, "ch": core}) for core in (0, 1)
    ]
    tell_peer.start()

    @pl.when(c == 1)
    def _():
        for copy in tell_next:
            copy.start()

    tell_peer.wait_recv()
    tell_next[0].wait_recv()
    lane = iota((EMB + 8, 128), 1)
    own = jnp.where(c == 0, msg[...], msg_peer[...])
    late = jnp.where(c == 0, msg_peer[...], msg[...])
    whole = jnp.where(lane < 32, msg_left[...], jnp.where(lane < 96, own, late))
    lat_ref[...] = whole[0:EMB, :]
    near_ref[...] = whole[EMB : EMB + 8, :]

    tell_peer.wait_send()
    for copy in sends:
        copy.wait_send()
    all_counts.wait_send()
    for i in (0, 1):
        first, count = pieces[i]
        mine, theirs = own_rows(i, first, count, jnp.where(c == 0, 416 + first, 1440 + first))
        mine().wait()
        theirs().wait()
        next_rows(2 + i, *pieces[2 + i])[0].wait_recv()

    @pl.when(c == 0)
    def _():
        for i in (2, 3):
            mine, theirs = own_rows(i, *pieces[i], 416 + pieces[i][0])
            mine().wait()
            theirs().wait_send()

    @pl.when(c == 1)
    def _():
        for copy in tell_next:
            copy.wait_send()
        for i in (2, 3):
            own_rows(i, *pieces[i], 416 + pieces[i][0])[1]().wait_recv()
            for copy in next_rows(i, *pieces[i]):
                copy.wait_send()


def hand_over(frames, latent, nearest, sharpest_out, latent_out, nearest_out, rows, columns, sem):
    def read(j):
        return pltpu.make_async_copy(frames.at[pl.ds(256 * j, 256)], rows.at[j], sem.at[0, j])

    def write(j):
        return pltpu.make_async_copy(columns.at[j], sharpest_out.at[:, pl.ds(256 * j, 256)], sem.at[1, j])

    for j in range(8):
        read(j).start()
    latent_out[...] = latent[...]
    nearest_out[...] = nearest[0]
    r, q = iota((256, 256), 0), iota((256, 256), 1)
    same, reverse = ones_where(r == q), ones_where(255 - r == q)
    for j in range(8):
        read(j).wait()
        to = 7 - j if 2 <= j < 6 else j
        for h in (0, 1):
            part = rows[j, :, 256 * h : 256 * (h + 1)]
            if to != j:
                part = nn(reverse, part).astype(BF)
            columns[to, 256 * h : 256 * (h + 1), :] = nt(same, part).astype(BF)
        write(to).start()
    for j in range(8):
        write(j).wait()


def on_device(samples, sample_counts, spaced, restore, shrinking, projector, dictionary):
    hbm = pl.BlockSpec(memory_space=pltpu.HBM)
    vmem = pl.BlockSpec(memory_space=pltpu.VMEM)
    dma = pltpu.SemaphoreType.DMA
    frames, latent, nearest = pl.pallas_call(
        kernel,
        out_shape=(
            jax.ShapeDtypeStruct((SHARD, H), BF),
            jax.ShapeDtypeStruct((EMB, 128), F32),
            jax.ShapeDtypeStruct((8, 128), F32),
        ),
        in_specs=[pl.BlockSpec(memory_space=pltpu.SMEM)] + [hbm] * 6,
        out_specs=(hbm, vmem, vmem),
        scratch_shapes=[
            pltpu.VMEM((CAP // 128, H, 128), BF),
            pltpu.VMEM((5, 3 * H, C), BF),
            pltpu.VMEM((5, C, H), BF),
            pltpu.VMEM((2, C, 4 * C), BF),
            pltpu.VMEM((3 * EMB, C), BF),
            pltpu.VMEM((EMB, BINS), F32),
            pltpu.VMEM((3 * EMB, BINS), BF),
            pltpu.VMEM((N_SEQ, 8, 128), I32),
            pltpu.VMEM((8, 128), I32),
            pltpu.VMEM((2, T, C), BF),
            pltpu.VMEM((2, T, H), BF),
            pltpu.VMEM((2, T, H), BF),
            pltpu.VMEM((2, EDGE, H), BF),
            pltpu.VMEM((PAD + 4 * T, C), BF),
            pltpu.VMEM((T, C), BF),
            pltpu.VMEM((HEAD + T + 8, 3 * H), F32),
            pltpu.VMEM((2, HEAD, 3 * H), F32),
            pltpu.VMEM((T, H), BF),
            pltpu.VMEM((8, 4 * T, 128), F32),
            pltpu.VMEM((T, 4 * C), BF),
            pltpu.VMEM((T, C), BF),
            pltpu.VMEM((T2, C), BF),
            pltpu.VMEM((EMB + 8, 128), F32),
            pltpu.VMEM((EMB + 8, 128), F32),
            pltpu.VMEM((EMB + 8, 128), F32),
            dma((31,)),
            dma((CAP // 128,)),
            dma((29,)),
            dma((29,)),
            dma((1,)),
            dma((1,)),
            dma((2, 2)),
            dma((2, 2)),
            dma((2,)),
            dma((2,)),
            dma((4,)),
            dma((4, 2)),
            dma((4,)),
            dma((2,)),
            dma((3,)),
            dma((2,)),
        ],
        compiler_params=pltpu.CompilerParams(
            collective_id=0, has_side_effects=True, vmem_limit_bytes=63 * 2**20
        ),
        name="encoder",
    )(sample_counts, samples, spaced, restore, shrinking, projector, dictionary)
    return pl.pallas_call(
        hand_over,
        out_shape=(
            jax.ShapeDtypeStruct((H, SHARD), BF),
            jax.ShapeDtypeStruct((EMB, 128), F32),
            jax.ShapeDtypeStruct((128,), F32),
        ),
        in_specs=[hbm, vmem, vmem],
        out_specs=(hbm, vmem, vmem),
        scratch_shapes=[pltpu.VMEM((8, 256, H), BF), pltpu.VMEM((8, H, 256), BF), dma((2, 8))],
        name="hand_over",
    )(frames, latent, nearest)


def solution(mesh):
    return jax.shard_map(
        on_device,
        mesh=mesh,
        in_specs=(
            P("ch", "seq"),
            P("seq"),
            P(None, None, "ch", None),
            P(None, None, "ch"),
            P(None, None, "ch", None),
            P(None, "ch"),
            P(),
        ),
        out_specs=(P("ch", "seq"), P(None, "seq"), P("seq")),
        check_vma=False,
    )
```

```python
import jax
import jax.numpy as jnp
from jax import lax
from jax.experimental import pallas as pl
from jax.experimental.pallas import tpu as pltpu
from jax.sharding import PartitionSpec as P

MESH = pl.DeviceIdType.MESH
BF, F32, I32 = jnp.bfloat16, jnp.float32, jnp.int32
C, H, EMB, BINS, SHARD, CAP = 1024, 512, 64, 2048, 2048, 3072
T = 304
T2 = 80
N_SEQ = 64
HEAD = 24
PAD = 32
EDGE = 2 * T


def nt(a, b):
    return lax.dot_general(a, b, (((1,), (1,)), ((), ())), preferred_element_type=F32)


def nn(a, b):
    return jnp.dot(a, b, preferred_element_type=F32)


def iota(shape, dim):
    return lax.broadcasted_iota(I32, shape, dim)


def ones_where(mask):
    return jnp.where(mask, 1.0, 0.0).astype(BF)


def kernel(
    cnt_ref, res_hbm, w1_hbm, w2_hbm, dn_hbm, pj_hbm, cb_hbm,
    out_hbm, lat_ref, near_ref,
    res, w1, w2, dn, pj, cb, cbk, counts, place, edge, send_r, send_rr, shift, x, a, pb, hid, y32, z, u, v,
    msg, msg_peer, msg_left,
    lsem, rsem, wsend, wrecv, csend, crecv, esend, erecv, hsend, hrecv, olocal, osend, opeer, oleft, msend, mrecv,
):
    s, c = lax.axis_index("seq"), lax.axis_index("ch")
    n_seq = lax.axis_size("seq")
    right, left = lax.rem(s + 1, n_seq), lax.rem(s + n_seq - 1, n_seq)
    other = 1 - c
    peer = {"seq": s, "ch": other}
    last = (s == n_seq - 1) & (c == 1)

    def remote(src, dst, send, recv, where):
        return pltpu.make_async_remote_copy(
            src_ref=src, dst_ref=dst, send_sem=send, recv_sem=recv, device_id=where, device_id_type=MESH
        )

    def weight(i, on):
        if i < 15:
            b, k = divmod(i, 3)
            tap = k + (1 - on) * (2 - 2 * k)
            return w1_hbm.at[b, k], w1.at[b, pl.ds(pl.multiple_of(512 * tap + 256 * c, 256), 256)]
        if i < 20:
            return w2_hbm.at[i - 15], w2.at[i - 15, :, pl.ds(pl.multiple_of(256 * c, 256), 256)]
        if i < 28:
            l, k = divmod(i - 20, 4)
            tap = k + (1 - on) * (3 - 2 * k)
            return dn_hbm.at[l, k], dn.at[
                l, pl.ds(pl.multiple_of(512 * c, 512), 512), pl.ds(pl.multiple_of(1024 * tap, 1024), 1024)
            ]
        return pj_hbm, pj.at[pl.ds(0, EMB), pl.ds(pl.multiple_of(512 * c, 512), 512)]

    def weight_local(i):
        return pltpu.make_async_copy(*weight(i, c), lsem.at[i])

    def weight_remote(i):
        return remote(*weight(i, other), wsend.at[i], wrecv.at[i], peer)

    def block_weights(b):
        return [3 * b, 3 * b + 1, 3 * b + 2, 15 + b]

    def down_weights(l):
        return [20 + 4 * l + k for k in range(4)]

    def need(items):
        for i in items:
            weight_local(i).wait()
            weight_remote(i).wait_recv()

    groups = [
        block_weights(0) + block_weights(1),
        down_weights(0) + block_weights(2),
        block_weights(3) + down_weights(1) + block_weights(4) + [28],
    ]
    load_res = [
        pltpu.make_async_copy(res_hbm.at[:, pl.ds(128 * k, 128)], res.at[k], rsem.at[k]) for k in range(CAP // 128)
    ]
    load_cb = pltpu.make_async_copy(cb_hbm, cb, lsem.at[30])
    for copy in load_res:
        copy.start()
    load_cb.start()

    barrier = pltpu.get_barrier_semaphore()
    def chip(q):
        return {"seq": lax.rem(s + q, n_seq), "ch": c}

    def greet(q, _):
        pl.semaphore_signal(barrier, inc=1, device_id=chip(q), device_id_type=MESH)
        return 0

    lax.fori_loop(1, N_SEQ, greet, 0)
    for where in (peer, {"seq": left, "ch": other}, {"seq": right, "ch": other}):
        pl.semaphore_signal(barrier, inc=1, device_id=where, device_id_type=MESH)

    cnt = cnt_ref[0]
    x[0:PAD, :] = jnp.zeros((PAD, C), BF)
    pb[...] = jnp.zeros(pb.shape, F32)

    def picked(first, sign):
        lowest = jnp.maximum(jnp.minimum(first, first + sign * (T - 1)), 0)
        tile = jnp.minimum(lax.shift_right_logical(lowest, 7), CAP // 128 - 4)
        column = 128 * tile + iota((T, 512), 1)
        pick = ones_where((column == first + sign * iota((T, 512), 0)) & (column < cnt))
        found = jnp.concatenate([res[tile + q] for q in range(4)], axis=1)
        return nt(pick, found).astype(BF)

    def tell_count(q, _):
        remote(counts.at[s], counts.at[s], csend.at[0], crecv.at[0], chip(q)).start()
        return 0

    others = pl.ds(0, N_SEQ - 1)
    all_counts = remote(counts.at[others], counts.at[others], csend.at[0], crecv.at[0], chip(1))

    half_c = pl.ds(pl.multiple_of(512 * c, 512), 512)
    sends = []

    def send_edges(m):
        for q, (buffer, where) in enumerate(
            ((send_r, {"seq": right, "ch": 0}), (send_rr, {"seq": left, "ch": 1}))
        ):
            copy = remote(buffer.at[m], edge.at[m, :, half_c], esend.at[m, q], erecv.at[m, c], where)
            copy.start()
            sends.append(copy)

    for copy in load_res:
        copy.wait()
    for i in groups[0]:
        weight_local(i).start()
    pl.semaphore_wait(barrier, N_SEQ + 2)
    counts[s] = jnp.full((8, 128), cnt, I32)
    lax.fori_loop(1, N_SEQ, tell_count, 0)
    send_r[0] = picked(cnt - 1, -1)
    send_rr[0] = picked(jnp.int32(0), 1)
    send_edges(0)
    for i in groups[0]:
        sends.append(weight_remote(i))
        sends[-1].start()
    send_r[1] = picked(cnt - 1 - T, -1)
    send_rr[1] = picked(jnp.int32(T), 1)
    send_edges(1)
    for g in (1, 2):
        for i in groups[g]:
            weight_local(i).start()
    all_counts.wait_recv()
    earlier = iota((N_SEQ, 8, 128), 0) < s
    place[...] = jnp.sum(jnp.where(earlier, counts[...], 0), axis=0) - SHARD * s
    offset = place[0, 0]
    gap = jnp.where(c == 0, SHARD // 2 - offset, offset + cnt - SHARD)

    def window(core, n):
        sign = 2 * core - 1
        first = jnp.where(core == 1, 1440, 1631) + sign * T * n - offset
        return picked(first, sign)

    def to_peer(h):
        rows = pl.ds(PAD + EDGE * h, EDGE)
        return remote(shift.at[h], x.at[rows, half_c], hsend.at[h], hrecv.at[h], peer)

    def place_half(h):
        def shifted(n, _):
            shift[h, pl.ds(pl.multiple_of(T * n, 16), T), :] = window(other, 2 * h + n)
            return 0

        lax.fori_loop(0, 2, shifted, 0)
        sends.append(to_peer(h))
        sends[-1].start()

        def placed(n, _):
            x[pl.ds(pl.multiple_of(PAD + EDGE * h + T * n, 16), T), half_c] = window(c, 2 * h + n)
            return 0

        lax.fori_loop(0, 2, placed, 0)

    place_half(0)
    for i in groups[1]:
        sends.append(weight_remote(i))
        sends[-1].start()

    def block(ref, at, rows, b, w, dilation, lag, bound, follow, wide_at):
        here = HEAD - lag

        def tap(j, k):
            def step():
                lanes = pl.ds(512 * k + 256 * j, 256)
                pb[w, HEAD : HEAD + rows, lanes] = nt(a[w, :rows, :], w1[b, lanes, :])

            return step

        def hide(n):
            def step():
                def product(k, start):
                    return pb[w, start : start + rows, pl.ds(512 * k + 128 * n, 128)]

                p0, p1, p2 = product(0, here - dilation), product(1, here), product(2, here + dilation)
                if bound is not None:
                    t = iota((rows, 128), 0) - jnp.where(last, bound, 1 << 20)
                    p0 = jnp.where((t >= 0) & (t < dilation), 0.0, p0)
                    p2 = jnp.where((t < 0) & (t >= -dilation), 0.0, p2)
                hid[w, :rows, pl.ds(128 * n, 128)] = jnp.maximum(p0 + p1 + p2, 0.0).astype(BF)

            return step

        def keep():
            if lag:
                pb[w, 0:HEAD, :] = pb[w, rows : rows + HEAD, :]

        def back(n):
            def step():
                lanes = pl.ds(256 * n, 256)
                update = nt(hid[w, :rows, :], w2[b, lanes, :])
                new = (ref[at : at + rows, lanes].astype(F32) + update).astype(BF)
                ref[at : at + rows, lanes] = new
                if follow is not None:
                    a[follow, :rows, lanes] = jnp.maximum(new, jnp.zeros((), BF))
                if wide_at is not None:
                    for q in (0, 1):
                        y32[2 * n + q, wide_at : wide_at + rows, :] = new[:, 128 * q : 128 * (q + 1)].astype(F32)

            return step

        taps = [tap(j, k) for j in range(2) for k in range(3)]
        return taps, [hide(n) for n in range(4)], [keep] + [back(n) for n in range(4)]

    def beside(*lists):
        longest = max(len(steps) for steps in lists)
        for i in range(longest):
            for steps in lists:
                for step in steps[len(steps) * i // longest : len(steps) * (i + 1) // longest]:
                    step()

    def alone(steps, filler=()):
        taps, hides, backs = steps
        beside(taps[:3], list(filler))
        beside(taps[3:], hides[:2])
        beside(hides[2:])
        beside(backs)

    def pair(first, second):
        beside(first[0])
        beside(second[0], first[1])
        beside(first[2], second[1])
        beside(second[2])

    def half(core):
        return pl.ds(pl.multiple_of(512 * core, 512), 512)

    def own_rows(i, first, count, start):
        rows, to = pl.ds(PAD + first, count), pl.ds(pl.multiple_of(start, 16), count)
        return (
            lambda: pltpu.make_async_copy(x.at[rows, half(c)], out_hbm.at[to], olocal.at[i]),
            lambda: remote(x.at[rows, half(other)], out_hbm.at[to], osend.at[i, 0], opeer.at[i], peer),
        )

    def next_rows(i, first, count):
        return [
            remote(
                x.at[pl.ds(PAD + first, count), pl.ds(512 * core, 512)],
                out_hbm.at[pl.ds(first - EDGE, count)],
                osend.at[i, core],
                oleft.at[i - 2],
                {"seq": right, "ch": core},
            )
            for core in (0, 1)
        ]

    pieces = ((96, 176), (272, 336), (608, 272), (880, 240))

    def emit(i):
        first, count = pieces[i]
        if i < 2:
            for copy in own_rows(i, first, count, jnp.where(c == 0, 416 + first, 1440 + first)):
                copy().start()
        else:

            @pl.when(c == 0)
            def _():
                for copy in own_rows(i, first, count, 416 + first):
                    copy().start()

            @pl.when(c == 1)
            def _():
                for copy in next_rows(i, first, count):
                    copy.start()

    def fold(first, rows):
        def one(n):
            def step():
                for k in range(4):
                    lanes = pl.ds(1024 * k + 128 * n, 128)
                    z[first : first + rows, lanes] = y32[n, pl.ds(4 * first + k, rows, stride=4), :].astype(BF)

            return step

        return [one(n) for n in range(8)]

    def finest(n, b):
        start = PAD + T * n - 16 * b
        bound = EDGE - (T * n - 16 * b - 16) if n == 2 else None
        return block(x, start - 16, T, b, b, (1, 3)[b], 16, bound, None if b else 1, T * n if b else None)

    def ready(n):
        at = PAD + T * n
        if n % 2 == 0:
            to_peer(n // 2).wait_recv()
        if n < 2:
            a[0] = jnp.maximum(x[at : at + T, :], jnp.zeros((), BF))
            return
        m = n - 2
        for core in (0, 1):
            remote(
                send_r.at[m], edge.at[m, :, pl.ds(512 * core, 512)], esend.at[m, 0], erecv.at[m, core],
                {"seq": right, "ch": 0},
            ).wait_recv()
        picks = [ones_where(T * e + iota((T, T), 1) == T * m + iota((T, T), 0) - gap) for e in range(m + 1)]
        for q in range(4):
            lanes = pl.ds(256 * q, 256)
            total = x[at : at + T, lanes].astype(F32)
            for e in range(m + 1):
                total = total + nn(picks[e], edge[e, :, lanes])
            full = total.astype(BF)
            x[at : at + T, lanes] = full
            a[0, :, lanes] = jnp.maximum(full, jnp.zeros((), BF))

    need(block_weights(0))
    ready(0)
    alone(finest(0, 0))
    for i in groups[2]:
        sends.append(weight_remote(i))
        sends[-1].start()
    need(block_weights(1))
    place_half(1)
    for n in range(3):
        ready(n + 1)
        pair(finest(n, 1), finest(n + 1, 0))
        for i in ((0,), (), (1, 2))[n]:
            emit(i)
    alone(finest(3, 1), fold(0, 208))
    emit(3)
    beside(fold(208, T - 208))

    need(down_weights(0))

    def down(l, rows, to):
        for n in range(4):
            lanes = pl.ds(256 * n, 256)
            new = nt(z[:rows, :], dn[l, lanes, :]).astype(BF)
            to[:, lanes] = new
            a[0, :rows, lanes] = jnp.maximum(new, jnp.zeros((), BF))

    down(0, T, u)
    need(block_weights(2))
    need(block_weights(3))
    alone(block(u, 0, T, 2, 0, 1, 0, 160, 1, None))
    alone(block(u, 0, T, 3, 1, 3, 0, 160, None, 0))

    beside(fold(0, T2))
    need(down_weights(1))
    need(block_weights(4))
    down(1, T2, v)
    alone(block(v, 0, T2, 4, 0, 3, 0, 40, None, None))

    need([28])
    load_cb.wait()
    pj[EMB : 2 * EMB, :] = pj[0:EMB, :]
    pj[2 * EMB : 3 * EMB, :] = pj[0:EMB, :]
    book = cb[...]
    book_hi = book.astype(BF)
    cbk[0:EMB, :] = book_hi
    cbk[EMB : 2 * EMB, :] = book_hi
    cbk[2 * EMB : 3 * EMB, :] = (book - book_hi.astype(F32)).astype(BF)
    book_sq = jnp.sum(book * book, axis=0, keepdims=True)
    frame, row = iota((128, T2), 0), iota((128, T2), 1)
    spot = jnp.where(c == 0, 103 - row, lax.rem(88 + row, 128))
    coarse = nn(ones_where((spot == frame) & (row >= 8) & (row < 72)), v[...]).astype(BF)
    latent = nt(pj[0:EMB, :], coarse)
    thrice = nt(coarse, pj[...])
    hi = thrice.astype(BF)
    lo = (thrice - hi.astype(F32)).astype(BF)
    lane = iota((128, 3 * EMB), 1)
    lhs = jnp.where((lane >= EMB) & (lane < 2 * EMB), lo, hi)
    nearest = jnp.full((128, 1), jnp.inf, F32)
    for q in range(4):
        columns = slice(512 * q, 512 * (q + 1))
        distance = book_sq[:, columns] - 2.0 * nn(lhs, cbk[:, columns])
        nearest = jnp.minimum(nearest, jnp.min(distance, axis=1, keepdims=True))
    diagonal = iota((128, 128), 0) == iota((128, 128), 1)
    nearest = jnp.sum(jnp.where(diagonal, nearest, 0.0), axis=0, keepdims=True)
    nearest = (nearest + jnp.sum(latent * latent, axis=0, keepdims=True)) * (1.0 / EMB)
    msg[0:EMB, :] = latent
    msg[EMB : EMB + 8, :] = jnp.broadcast_to(nearest, (8, 128))
    tell_peer = remote(msg, msg_peer, msend.at[0], mrecv.at[0], peer)
    tell_next = [
        remote(msg, msg_left, msend.at[1 + core], mrecv.at[1], {"seq": right, "ch": core}) for core in (0, 1)
    ]
    tell_peer.start()

    @pl.when(c == 1)
    def _():
        for copy in tell_next:
            copy.start()

    tell_peer.wait_recv()
    tell_next[0].wait_recv()
    lane = iota((EMB + 8, 128), 1)
    own = jnp.where(c == 0, msg[...], msg_peer[...])
    late = jnp.where(c == 0, msg_peer[...], msg[...])
    whole = jnp.where(lane < 32, msg_left[...], jnp.where(lane < 96, own, late))
    lat_ref[...] = whole[0:EMB, :]
    near_ref[...] = whole[EMB : EMB + 8, :]

    tell_peer.wait_send()
    for copy in sends:
        copy.wait_send()
    all_counts.wait_send()
    for i in (0, 1):
        first, count = pieces[i]
        mine, theirs = own_rows(i, first, count, jnp.where(c == 0, 416 + first, 1440 + first))
        mine().wait()
        theirs().wait()
        next_rows(2 + i, *pieces[2 + i])[0].wait_recv()

    @pl.when(c == 0)
    def _():
        for i in (2, 3):
            mine, theirs = own_rows(i, *pieces[i], 416 + pieces[i][0])
            mine().wait()
            theirs().wait_send()

    @pl.when(c == 1)
    def _():
        for copy in tell_next:
            copy.wait_send()
        for i in (2, 3):
            own_rows(i, *pieces[i], 416 + pieces[i][0])[1]().wait_recv()
            for copy in next_rows(i, *pieces[i]):
                copy.wait_send()


def hand_over(frames, latent, nearest, sharpest_out, latent_out, nearest_out, rows, columns, sem):
    def read(j):
        return pltpu.make_async_copy(frames.at[pl.ds(256 * j, 256)], rows.at[j], sem.at[0, j])

    def write(j):
        return pltpu.make_async_copy(columns.at[j], sharpest_out.at[:, pl.ds(256 * j, 256)], sem.at[1, j])

    for j in range(8):
        read(j).start()
    latent_out[...] = latent[...]
    nearest_out[...] = nearest[0]
    r, q = iota((256, 256), 0), iota((256, 256), 1)
    same, reverse = ones_where(r == q), ones_where(255 - r == q)
    for j in range(8):
        read(j).wait()

    def turned(j, to):
        for h in (0, 1):
            part = rows[j, :, 256 * h : 256 * (h + 1)]
            if to != j:
                part = nn(reverse, part).astype(BF)
            columns[to, 256 * h : 256 * (h + 1), :] = nt(same, part).astype(BF)

    for group in ((0, 1, 6, 7), (2, 3, 4, 5)):
        for j in group:
            turned(j, 7 - j if 2 <= j < 6 else j)
        for j in group:
            write(j).start()
    for j in range(8):
        write(j).wait()


def on_device(samples, sample_counts, spaced, restore, shrinking, projector, dictionary):
    hbm = pl.BlockSpec(memory_space=pltpu.HBM)
    vmem = pl.BlockSpec(memory_space=pltpu.VMEM)
    dma = pltpu.SemaphoreType.DMA
    frames, latent, nearest = pl.pallas_call(
        kernel,
        out_shape=(
            jax.ShapeDtypeStruct((SHARD, H), BF),
            jax.ShapeDtypeStruct((EMB, 128), F32),
            jax.ShapeDtypeStruct((8, 128), F32),
        ),
        in_specs=[pl.BlockSpec(memory_space=pltpu.SMEM)] + [hbm] * 6,
        out_specs=(hbm, vmem, vmem),
        scratch_shapes=[
            pltpu.VMEM((CAP // 128, H, 128), BF),
            pltpu.VMEM((5, 3 * H, C), BF),
            pltpu.VMEM((5, C, H), BF),
            pltpu.VMEM((2, C, 4 * C), BF),
            pltpu.VMEM((3 * EMB, C), BF),
            pltpu.VMEM((EMB, BINS), F32),
            pltpu.VMEM((3 * EMB, BINS), BF),
            pltpu.VMEM((N_SEQ, 8, 128), I32),
            pltpu.VMEM((8, 128), I32),
            pltpu.VMEM((2, T, C), BF),
            pltpu.VMEM((2, T, H), BF),
            pltpu.VMEM((2, T, H), BF),
            pltpu.VMEM((2, EDGE, H), BF),
            pltpu.VMEM((PAD + 4 * T, C), BF),
            pltpu.VMEM((2, T, C), BF),
            pltpu.VMEM((2, HEAD + T + 8, 3 * H), F32),
            pltpu.VMEM((2, T, H), BF),
            pltpu.VMEM((8, 4 * T, 128), F32),
            pltpu.VMEM((T, 4 * C), BF),
            pltpu.VMEM((T, C), BF),
            pltpu.VMEM((T2, C), BF),
            pltpu.VMEM((EMB + 8, 128), F32),
            pltpu.VMEM((EMB + 8, 128), F32),
            pltpu.VMEM((EMB + 8, 128), F32),
            dma((31,)),
            dma((CAP // 128,)),
            dma((29,)),
            dma((29,)),
            dma((1,)),
            dma((1,)),
            dma((2, 2)),
            dma((2, 2)),
            dma((2,)),
            dma((2,)),
            dma((4,)),
            dma((4, 2)),
            dma((4,)),
            dma((2,)),
            dma((3,)),
            dma((2,)),
        ],
        compiler_params=pltpu.CompilerParams(
            collective_id=0, has_side_effects=True, vmem_limit_bytes=63 * 2**20
        ),
        name="encoder",
    )(sample_counts, samples, spaced, restore, shrinking, projector, dictionary)
    return pl.pallas_call(
        hand_over,
        out_shape=(
            jax.ShapeDtypeStruct((H, SHARD), BF),
            jax.ShapeDtypeStruct((EMB, 128), F32),
            jax.ShapeDtypeStruct((128,), F32),
        ),
        in_specs=[hbm, vmem, vmem],
        out_specs=(hbm, vmem, vmem),
        scratch_shapes=[pltpu.VMEM((8, 256, H), BF), pltpu.VMEM((8, H, 256), BF), dma((2, 8))],
        name="hand_over",
    )(frames, latent, nearest)


def solution(mesh):
    return jax.shard_map(
        on_device,
        mesh=mesh,
        in_specs=(
            P("ch", "seq"),
            P("seq"),
            P(None, None, "ch", None),
            P(None, None, "ch"),
            P(None, None, "ch", None),
            P(None, "ch"),
            P(),
        ),
        out_specs=(P("ch", "seq"), P(None, "seq"), P("seq")),
        check_vma=False,
    )
```

```python
import jax
import jax.numpy as jnp
from jax import lax
from jax.experimental import pallas as pl
from jax.experimental.pallas import tpu as pltpu
from jax.sharding import PartitionSpec as P

MESH = pl.DeviceIdType.MESH
BF, F32, I32 = jnp.bfloat16, jnp.float32, jnp.int32
C, H, EMB, BINS, SHARD, CAP = 1024, 512, 64, 2048, 2048, 3072
T = 304
T2 = 80
N_SEQ = 64
HEAD = 24
PAD = 32
EDGE = 2 * T


def aligned(at, step):
    return at if isinstance(at, int) else pl.multiple_of(at, step)


def nt(a, b):
    return lax.dot_general(a, b, (((1,), (1,)), ((), ())), preferred_element_type=F32)


def nn(a, b):
    return jnp.dot(a, b, preferred_element_type=F32)


def iota(shape, dim):
    return lax.broadcasted_iota(I32, shape, dim)


def ones_where(mask):
    return jnp.where(mask, 1.0, 0.0).astype(BF)


def kernel(
    cnt_ref, res_hbm, w1_hbm, w2_hbm, dn_hbm, pj_hbm, cb_hbm,
    out_hbm, lat_ref, near_ref,
    res, w1, w2, dn, pj, cb, cbk, counts, place, edge, send_r, send_rr, shift, x, a, pb, hid, y32, z, u, v,
    msg, msg_peer, msg_left,
    lsem, rsem, wsend, wrecv, csend, crecv, esend, erecv, hsend, hrecv, olocal, osend, opeer, oleft, msend, mrecv,
):
    s, c = lax.axis_index("seq"), lax.axis_index("ch")
    n_seq = lax.axis_size("seq")
    right, left = lax.rem(s + 1, n_seq), lax.rem(s + n_seq - 1, n_seq)
    other = 1 - c
    peer = {"seq": s, "ch": other}
    last = (s == n_seq - 1) & (c == 1)

    def remote(src, dst, send, recv, where):
        return pltpu.make_async_remote_copy(
            src_ref=src, dst_ref=dst, send_sem=send, recv_sem=recv, device_id=where, device_id_type=MESH
        )

    def weight(i, on):
        if i < 15:
            b, k = divmod(i, 3)
            tap = k + (1 - on) * (2 - 2 * k)
            return w1_hbm.at[b, k], w1.at[b, pl.ds(aligned(512 * tap + 256 * c, 256), 256)]
        if i < 20:
            return w2_hbm.at[i - 15], w2.at[i - 15, :, pl.ds(aligned(256 * c, 256), 256)]
        if i < 28:
            l, k = divmod(i - 20, 4)
            tap = k + (1 - on) * (3 - 2 * k)
            return dn_hbm.at[l, k], dn.at[
                l, pl.ds(aligned(512 * c, 512), 512), pl.ds(aligned(1024 * tap, 1024), 1024)
            ]
        return pj_hbm, pj.at[pl.ds(0, EMB), pl.ds(aligned(512 * c, 512), 512)]

    def weight_local(i):
        return pltpu.make_async_copy(*weight(i, c), lsem.at[i])

    def weight_remote(i):
        return remote(*weight(i, other), wsend.at[i], wrecv.at[i], peer)

    def block_weights(b):
        return [3 * b, 3 * b + 1, 3 * b + 2, 15 + b]

    def down_weights(l):
        return [20 + 4 * l + k for k in range(4)]

    def need(items):
        for i in items:
            weight_local(i).wait()
            weight_remote(i).wait_recv()

    groups = [
        block_weights(0) + block_weights(1),
        down_weights(0) + block_weights(2),
        block_weights(3) + down_weights(1) + block_weights(4) + [28],
    ]
    load_res = [
        pltpu.make_async_copy(res_hbm.at[:, pl.ds(128 * k, 128)], res.at[k], rsem.at[k]) for k in range(CAP // 128)
    ]
    load_cb = pltpu.make_async_copy(cb_hbm, cb, lsem.at[30])
    for copy in load_res:
        copy.start()
    load_cb.start()

    barrier = pltpu.get_barrier_semaphore()
    def chip(q):
        return {"seq": lax.rem(s + q, n_seq), "ch": c}

    def greet(q, _):
        pl.semaphore_signal(barrier, inc=1, device_id=chip(q), device_id_type=MESH)
        return 0

    lax.fori_loop(1, N_SEQ, greet, 0)
    for where in (peer, {"seq": left, "ch": other}, {"seq": right, "ch": other}):
        pl.semaphore_signal(barrier, inc=1, device_id=where, device_id_type=MESH)

    cnt = cnt_ref[0]
    x[0:PAD, :] = jnp.zeros((PAD, C), BF)
    pb[...] = jnp.zeros(pb.shape, F32)

    def picked(first, sign):
        lowest = jnp.maximum(jnp.minimum(first, first + sign * (T - 1)), 0)
        tile = jnp.minimum((lowest >> 7), CAP // 128 - 4)
        column = 128 * tile + iota((T, 512), 1)
        pick = ones_where((column == first + sign * iota((T, 512), 0)) & (column < cnt))
        found = jnp.concatenate([res[tile + q] for q in range(4)], axis=1)
        return nt(pick, found).astype(BF)

    def tell_count(q, _):
        remote(counts.at[s], counts.at[s], csend.at[0], crecv.at[0], chip(q)).start()
        return 0

    others = pl.ds(0, N_SEQ - 1)
    all_counts = remote(counts.at[others], counts.at[others], csend.at[0], crecv.at[0], chip(1))

    half_c = pl.ds(aligned(512 * c, 512), 512)
    sends = []

    def send_edges(m):
        for q, (buffer, where) in enumerate(
            ((send_r, {"seq": right, "ch": 0}), (send_rr, {"seq": left, "ch": 1}))
        ):
            copy = remote(buffer.at[m], edge.at[m, :, half_c], esend.at[m, q], erecv.at[m, c], where)
            copy.start()
            sends.append(copy)

    for copy in load_res:
        copy.wait()
    for i in groups[0]:
        weight_local(i).start()
    pl.semaphore_wait(barrier, N_SEQ + 2)
    counts[s] = jnp.full((8, 128), cnt, I32)
    lax.fori_loop(1, N_SEQ, tell_count, 0)
    send_r[0] = picked(cnt - 1, -1)
    send_rr[0] = picked(0 * cnt, 1)
    send_edges(0)
    for i in groups[0]:
        sends.append(weight_remote(i))
        sends[-1].start()
    send_r[1] = picked(cnt - 1 - T, -1)
    send_rr[1] = picked(0 * cnt + T, 1)
    send_edges(1)
    for g in (1, 2):
        for i in groups[g]:
            weight_local(i).start()
    all_counts.wait_recv()
    earlier = iota((N_SEQ, 8, 128), 0) < s
    place[...] = jnp.sum(jnp.where(earlier, counts[...], 0), axis=0) - SHARD * s
    offset = place[0, 0]
    gap = jnp.where(c == 0, SHARD // 2 - offset, offset + cnt - SHARD)

    def window(core, n):
        sign = 2 * core - 1
        first = 1631 - 191 * core + sign * T * n - offset
        return picked(first, sign)

    def to_peer(h):
        rows = pl.ds(PAD + EDGE * h, EDGE)
        return remote(shift.at[h], x.at[rows, half_c], hsend.at[h], hrecv.at[h], peer)

    def place_half(h):
        def shifted(n, _):
            shift[h, pl.ds(aligned(T * n, 16), T), :] = window(other, 2 * h + n)
            return 0

        lax.fori_loop(0, 2, shifted, 0)
        to_peer(h).start()

        def placed(n, _):
            x[pl.ds(aligned(PAD + EDGE * h + T * n, 16), T), half_c] = window(c, 2 * h + n)
            return 0

        lax.fori_loop(0, 2, placed, 0)

    place_half(0)
    for i in groups[1]:
        sends.append(weight_remote(i))
        sends[-1].start()

    def block(ref, at, rows, b, w, hide, lag, wide_at):
        for n in range(6):
            lanes = pl.ds(256 * n, 256)
            pb[w, HEAD : HEAD + rows, lanes] = nt(a[w, :rows, :], w1[b, lanes, :])
        hide()
        if lag:
            pb[w, 0:HEAD, :] = pb[w, rows : rows + HEAD, :]
        for n in range(4):
            lanes = pl.ds(256 * n, 256)
            update = nt(hid[:rows, :], w2[b, lanes, :])
            new = (ref[pl.ds(at, rows), lanes].astype(F32) + update).astype(BF)
            ref[pl.ds(at, rows), lanes] = new
            a[1 - w, :rows, lanes] = jnp.maximum(new, jnp.zeros((), BF))
            for q in (0, 1):
                y32[2 * n + q, pl.ds(wide_at, rows), :] = new[:, 128 * q : 128 * (q + 1)].astype(F32)

    def hidden(first, rows, w, dilation, lag, bound=None):
        here = HEAD - lag + first
        for n in range(4):

            def product(k, start):
                return pb[w, start : start + rows, pl.ds(512 * k + 128 * n, 128)]

            p0, p1, p2 = product(0, here - dilation), product(1, here), product(2, here + dilation)
            if bound is not None:
                t = iota((rows, 128), 0) + (first - bound)
                p0 = jnp.where((t >= 0) & (t < dilation), 0.0, p0)
                p2 = jnp.where((t < 0) & (t >= -dilation), 0.0, p2)
            hid[first : first + rows, pl.ds(128 * n, 128)] = jnp.maximum(p0 + p1 + p2, 0.0).astype(BF)

    def hidden_at(rows, w, dilation, lag, bound, here=None):
        hidden(0, rows, w, dilation, lag)

        @pl.when(last if here is None else last & here)
        def _():
            hidden(bound // 16 * 16 - 16, 48, w, dilation, lag, bound)

    def half(core):
        return pl.ds(aligned(512 * core, 512), 512)

    def own_rows(i, first, count, start):
        rows, to = pl.ds(PAD + first, count), pl.ds(aligned(start, 16), count)
        return (
            lambda: pltpu.make_async_copy(x.at[rows, half(c)], out_hbm.at[to], olocal.at[i]),
            lambda: remote(x.at[rows, half(other)], out_hbm.at[to], osend.at[i, 0], opeer.at[i], peer),
        )

    def next_rows(i, first, count):
        return [
            remote(
                x.at[pl.ds(PAD + first, count), pl.ds(512 * core, 512)],
                out_hbm.at[pl.ds(first - EDGE, count)],
                osend.at[i, core],
                oleft.at[i - 2],
                {"seq": right, "ch": core},
            )
            for core in (0, 1)
        ]

    pieces = ((96, 176), (272, 336), (608, 272), (880, 240))

    def emit(i):
        first, count = pieces[i]
        if i < 2:
            for copy in own_rows(i, first, count, 416 + first + 1024 * c):
                copy().start()
        else:

            @pl.when(c == 0)
            def _():
                for copy in own_rows(i, first, count, 416 + first):
                    copy().start()

            @pl.when(c == 1)
            def _():
                for copy in next_rows(i, first, count):
                    copy.start()

    def fold(rows):
        for n in range(8):
            for k in range(4):
                lanes = pl.ds(1024 * k + 128 * n, 128)
                z[:rows, lanes] = y32[n, pl.ds(k, rows, stride=4), :].astype(BF)

    def ready(n):
        at = PAD + T * n
        if n % 2 == 0:
            to_peer(n // 2).wait_recv()
        if n < 2:
            a[0] = jnp.maximum(x[at : at + T, :], jnp.zeros((), BF))
            return
        m = n - 2
        for core in (0, 1):
            remote(
                send_r.at[m], edge.at[m, :, pl.ds(512 * core, 512)], esend.at[m, 0], erecv.at[m, core],
                {"seq": right, "ch": 0},
            ).wait_recv()
        picks = [ones_where(T * e + iota((T, T), 1) == T * m + iota((T, T), 0) - gap) for e in range(m + 1)]
        for q in range(4):
            lanes = pl.ds(256 * q, 256)
            total = x[at : at + T, lanes].astype(F32)
            for e in range(m + 1):
                total = total + nn(picks[e], edge[e, :, lanes])
            full = total.astype(BF)
            x[at : at + T, lanes] = full
            a[0, :, lanes] = jnp.maximum(full, jnp.zeros((), BF))

    need(block_weights(0))
    need(block_weights(1))

    def finest(i, _):
        n, b = i >> 1, i & 1
        for chunk in range(4):

            @pl.when(i == 2 * chunk)
            def _():
                if chunk == 1:
                    place_half(1)
                    for g in groups[2]:
                        weight_remote(g).start()
                ready(chunk)

        def hide():
            for which in (0, 1):

                @pl.when(b == which)
                def _():
                    hidden_at(T, which, (1, 3)[which], 16, 16 + 16 * which, n == 2)

        at = aligned(PAD + T * n - 16 * b - 16, 16)
        block(x, at, T, b, b, hide, 16, aligned(T * n, 16))
        for chunk, ones in enumerate(((0,), (), (1, 2), (3,))):
            if ones:

                @pl.when(i == 2 * chunk + 1)
                def _():
                    for one in ones:
                        emit(one)

        return 0

    lax.fori_loop(0, 8, finest, 0)
    sends += [weight_remote(g) for g in groups[2]] + [to_peer(0), to_peer(1)]

    fold(T)
    need(down_weights(0))

    def down(l, rows, to):
        for n in range(4):
            lanes = pl.ds(256 * n, 256)
            new = nt(z[:rows, :], dn[l, lanes, :]).astype(BF)
            to[:, lanes] = new
            a[0, :rows, lanes] = jnp.maximum(new, jnp.zeros((), BF))

    down(0, T, u)
    need(block_weights(2))
    need(block_weights(3))

    def middle(b, _):
        def hide():
            for which in (0, 1):

                @pl.when(b == which)
                def _():
                    hidden_at(T, which, (1, 3)[which], 0, 160)

        block(u, 0, T, 2 + b, b, hide, 0, 0)
        return 0

    lax.fori_loop(0, 2, middle, 0)

    fold(T2)
    need(down_weights(1))
    need(block_weights(4))
    down(1, T2, v)
    block(v, 0, T2, 4, 0, lambda: hidden_at(T2, 0, 3, 0, 40), 0, 0)

    need([28])
    load_cb.wait()
    pj[EMB : 2 * EMB, :] = pj[0:EMB, :]
    pj[2 * EMB : 3 * EMB, :] = pj[0:EMB, :]
    book = cb[...]
    book_hi = book.astype(BF)
    cbk[0:EMB, :] = book_hi
    cbk[EMB : 2 * EMB, :] = book_hi
    cbk[2 * EMB : 3 * EMB, :] = (book - book_hi.astype(F32)).astype(BF)
    book_sq = jnp.sum(book * book, axis=0, keepdims=True)
    frame, row = iota((128, T2), 0), iota((128, T2), 1)
    spot = jnp.where(c == 0, 103 - row, lax.rem(88 + row, 128))
    coarse = nn(ones_where((spot == frame) & (row >= 8) & (row < 72)), v[...]).astype(BF)
    latent = nt(pj[0:EMB, :], coarse)
    thrice = nt(coarse, pj[...])
    hi = thrice.astype(BF)
    lo = (thrice - hi.astype(F32)).astype(BF)
    lane = iota((128, 3 * EMB), 1)
    lhs = jnp.where((lane >= EMB) & (lane < 2 * EMB), lo, hi)
    nearest = jnp.full((128, 1), jnp.inf, F32)
    for q in range(4):
        columns = slice(512 * q, 512 * (q + 1))
        distance = book_sq[:, columns] - 2.0 * nn(lhs, cbk[:, columns])
        nearest = jnp.minimum(nearest, jnp.min(distance, axis=1, keepdims=True))
    diagonal = iota((128, 128), 0) == iota((128, 128), 1)
    nearest = jnp.sum(jnp.where(diagonal, nearest, 0.0), axis=0, keepdims=True)
    nearest = (nearest + jnp.sum(latent * latent, axis=0, keepdims=True)) * (1.0 / EMB)
    msg[0:EMB, :] = latent
    msg[EMB : EMB + 8, :] = jnp.broadcast_to(nearest, (8, 128))
    tell_peer = remote(msg, msg_peer, msend.at[0], mrecv.at[0], peer)
    tell_next = [
        remote(msg, msg_left, msend.at[1 + core], mrecv.at[1], {"seq": right, "ch": core}) for core in (0, 1)
    ]
    tell_peer.start()

    @pl.when(c == 1)
    def _():
        for copy in tell_next:
            copy.start()

    tell_peer.wait_recv()
    tell_next[0].wait_recv()
    lane = iota((EMB + 8, 128), 1)
    own = jnp.where(c == 0, msg[...], msg_peer[...])
    late = jnp.where(c == 0, msg_peer[...], msg[...])
    whole = jnp.where(lane < 32, msg_left[...], jnp.where(lane < 96, own, late))
    lat_ref[...] = whole[0:EMB, :]
    near_ref[...] = whole[EMB : EMB + 8, :]

    tell_peer.wait_send()
    for copy in sends:
        copy.wait_send()
    all_counts.wait_send()
    for i in (0, 1):
        first, count = pieces[i]
        mine, theirs = own_rows(i, first, count, 416 + first + 1024 * c)
        mine().wait()
        theirs().wait()
        next_rows(2 + i, *pieces[2 + i])[0].wait_recv()

    @pl.when(c == 0)
    def _():
        for i in (2, 3):
            mine, theirs = own_rows(i, *pieces[i], 416 + pieces[i][0])
            mine().wait()
            theirs().wait_send()

    @pl.when(c == 1)
    def _():
        for copy in tell_next:
            copy.wait_send()
        for i in (2, 3):
            own_rows(i, *pieces[i], 416 + pieces[i][0])[1]().wait_recv()
            for copy in next_rows(i, *pieces[i]):
                copy.wait_send()


def hand_over(frames, latent, nearest, sharpest_out, latent_out, nearest_out, rows, columns, sem):
    def read(j):
        return pltpu.make_async_copy(frames.at[pl.ds(256 * j, 256)], rows.at[j], sem.at[0, j])

    def write(j):
        return pltpu.make_async_copy(columns.at[j], sharpest_out.at[:, pl.ds(256 * j, 256)], sem.at[1, j])

    for j in range(8):
        read(j).start()
    latent_out[...] = latent[...]
    nearest_out[...] = nearest[0]
    r, q = iota((256, 256), 0), iota((256, 256), 1)
    same, reverse = ones_where(r == q), ones_where(255 - r == q)
    for j in range(8):
        read(j).wait()

    def turned(j, to):
        for h in (0, 1):
            part = rows[j, :, 256 * h : 256 * (h + 1)]
            if to != j:
                part = nn(reverse, part).astype(BF)
            columns[to, 256 * h : 256 * (h + 1), :] = nt(same, part).astype(BF)

    for group in ((0, 1, 6, 7), (2, 3, 4, 5)):
        for j in group:
            turned(j, 7 - j if 2 <= j < 6 else j)
        for j in group:
            write(j).start()
    for j in range(8):
        write(j).wait()


def on_device(samples, sample_counts, spaced, restore, shrinking, projector, dictionary):
    hbm = pl.BlockSpec(memory_space=pltpu.HBM)
    vmem = pl.BlockSpec(memory_space=pltpu.VMEM)
    dma = pltpu.SemaphoreType.DMA
    frames, latent, nearest = pl.pallas_call(
        kernel,
        out_shape=(
            jax.ShapeDtypeStruct((SHARD, H), BF),
            jax.ShapeDtypeStruct((EMB, 128), F32),
            jax.ShapeDtypeStruct((8, 128), F32),
        ),
        in_specs=[pl.BlockSpec(memory_space=pltpu.SMEM)] + [hbm] * 6,
        out_specs=(hbm, vmem, vmem),
        scratch_shapes=[
            pltpu.VMEM((CAP // 128, H, 128), BF),
            pltpu.VMEM((5, 3 * H, C), BF),
            pltpu.VMEM((5, C, H), BF),
            pltpu.VMEM((2, C, 4 * C), BF),
            pltpu.VMEM((3 * EMB, C), BF),
            pltpu.VMEM((EMB, BINS), F32),
            pltpu.VMEM((3 * EMB, BINS), BF),
            pltpu.VMEM((N_SEQ, 8, 128), I32),
            pltpu.VMEM((8, 128), I32),
            pltpu.VMEM((2, T, C), BF),
            pltpu.VMEM((2, T, H), BF),
            pltpu.VMEM((2, T, H), BF),
            pltpu.VMEM((2, EDGE, H), BF),
            pltpu.VMEM((PAD + 4 * T, C), BF),
            pltpu.VMEM((2, T, C), BF),
            pltpu.VMEM((2, HEAD + T + 8, 3 * H), F32),
            pltpu.VMEM((T, H), BF),
            pltpu.VMEM((8, 4 * T, 128), F32),
            pltpu.VMEM((T, 4 * C), BF),
            pltpu.VMEM((T, C), BF),
            pltpu.VMEM((T2, C), BF),
            pltpu.VMEM((EMB + 8, 128), F32),
            pltpu.VMEM((EMB + 8, 128), F32),
            pltpu.VMEM((EMB + 8, 128), F32),
            dma((31,)),
            dma((CAP // 128,)),
            dma((29,)),
            dma((29,)),
            dma((1,)),
            dma((1,)),
            dma((2, 2)),
            dma((2, 2)),
            dma((2,)),
            dma((2,)),
            dma((4,)),
            dma((4, 2)),
            dma((4,)),
            dma((2,)),
            dma((3,)),
            dma((2,)),
        ],
        compiler_params=pltpu.CompilerParams(
            collective_id=0, has_side_effects=True, vmem_limit_bytes=63 * 2**20
        ),
        name="encoder",
    )(sample_counts, samples, spaced, restore, shrinking, projector, dictionary)
    return pl.pallas_call(
        hand_over,
        out_shape=(
            jax.ShapeDtypeStruct((H, SHARD), BF),
            jax.ShapeDtypeStruct((EMB, 128), F32),
            jax.ShapeDtypeStruct((128,), F32),
        ),
        in_specs=[hbm, vmem, vmem],
        out_specs=(hbm, vmem, vmem),
        scratch_shapes=[pltpu.VMEM((8, 256, H), BF), pltpu.VMEM((8, H, 256), BF), dma((2, 8))],
        name="hand_over",
    )(frames, latent, nearest)


def solution(mesh):
    return jax.shard_map(
        on_device,
        mesh=mesh,
        in_specs=(
            P("ch", "seq"),
            P("seq"),
            P(None, None, "ch", None),
            P(None, None, "ch"),
            P(None, None, "ch", None),
            P(None, "ch"),
            P(),
        ),
        out_specs=(P("ch", "seq"), P(None, "seq"), P("seq")),
        check_vma=False,
    )
```

```python
import jax
import jax.numpy as jnp
from jax import lax
from jax.experimental import pallas as pl
from jax.experimental.pallas import tpu as pltpu
from jax.sharding import PartitionSpec as P

MESH = pl.DeviceIdType.MESH
BF, F32, I32 = jnp.bfloat16, jnp.float32, jnp.int32
C, H, EMB, BINS, SHARD, CAP = 1024, 512, 64, 2048, 2048, 3072
T = 304
T2 = 80
N_SEQ = 64
HEAD = 24
PAD = 32
EDGE = 2 * T


def nt(a, b):
    return lax.dot_general(a, b, (((1,), (1,)), ((), ())), preferred_element_type=F32)


def nn(a, b):
    return jnp.dot(a, b, preferred_element_type=F32)


def iota(shape, dim):
    return lax.broadcasted_iota(I32, shape, dim)


def ones_where(mask):
    return jnp.where(mask, 1.0, 0.0).astype(BF)


def kernel(
    cnt_ref, res_hbm, w1_hbm, w2_hbm, dn_hbm, pj_hbm, cb_hbm,
    out_hbm, lat_ref, near_ref,
    res, w1, w2, dn, pj, cb, cbk, counts, place, edge, send_r, send_rr, shift, x, a, pb, hid, y32, z, u, v,
    msg, msg_peer, msg_left,
    lsem, rsem, wsend, wrecv, csend, crecv, esend, erecv, hsend, hrecv, olocal, osend, opeer, oleft, msend, mrecv,
):
    s, c = lax.axis_index("seq"), lax.axis_index("ch")
    n_seq = lax.axis_size("seq")
    right, left = lax.rem(s + 1, n_seq), lax.rem(s + n_seq - 1, n_seq)
    other = 1 - c
    peer = {"seq": s, "ch": other}
    last = (s == n_seq - 1) & (c == 1)

    def remote(src, dst, send, recv, where):
        return pltpu.make_async_remote_copy(
            src_ref=src, dst_ref=dst, send_sem=send, recv_sem=recv, device_id=where, device_id_type=MESH
        )

    def weight(i, on):
        if i < 15:
            b, k = divmod(i, 3)
            tap = k + (1 - on) * (2 - 2 * k)
            return w1_hbm.at[b, k], w1.at[b, pl.ds(pl.multiple_of(512 * tap + 256 * c, 256), 256)]
        if i < 20:
            return w2_hbm.at[i - 15], w2.at[i - 15, :, pl.ds(pl.multiple_of(256 * c, 256), 256)]
        if i < 28:
            l, k = divmod(i - 20, 4)
            tap = k + (1 - on) * (3 - 2 * k)
            return dn_hbm.at[l, k], dn.at[
                l, pl.ds(pl.multiple_of(512 * c, 512), 512), pl.ds(pl.multiple_of(1024 * tap, 1024), 1024)
            ]
        return pj_hbm, pj.at[pl.ds(0, EMB), pl.ds(pl.multiple_of(512 * c, 512), 512)]

    def weight_local(i):
        return pltpu.make_async_copy(*weight(i, c), lsem.at[i])

    def weight_remote(i):
        return remote(*weight(i, other), wsend.at[i], wrecv.at[i], peer)

    def block_weights(b):
        return [3 * b, 3 * b + 1, 3 * b + 2, 15 + b]

    def down_weights(l):
        return [20 + 4 * l + k for k in range(4)]

    def need(items):
        for i in items:
            weight_local(i).wait()
            weight_remote(i).wait_recv()

    groups = [
        block_weights(0) + block_weights(1),
        down_weights(0) + block_weights(2),
        block_weights(3) + down_weights(1) + block_weights(4) + [28],
    ]
    load_res = [
        pltpu.make_async_copy(res_hbm.at[:, pl.ds(128 * k, 128)], res.at[k], rsem.at[k]) for k in range(CAP // 128)
    ]
    load_cb = pltpu.make_async_copy(cb_hbm, cb, lsem.at[30])
    barrier = pltpu.get_barrier_semaphore()
    def chip(q):
        return {"seq": lax.rem(s + q, n_seq), "ch": c}

    def greet(q, _):
        pl.semaphore_signal(barrier, inc=1, device_id=chip(q), device_id_type=MESH)
        return 0

    lax.fori_loop(1, N_SEQ, greet, 0)
    for where in (peer, {"seq": left, "ch": other}, {"seq": right, "ch": other}):
        pl.semaphore_signal(barrier, inc=1, device_id=where, device_id_type=MESH)
    for copy in load_res:
        copy.start()
    load_cb.start()

    cnt = cnt_ref[0]
    x[0:PAD, :] = jnp.zeros((PAD, C), BF)
    pb[...] = jnp.zeros(pb.shape, F32)

    def picked(first, sign):
        lowest = jnp.maximum(jnp.minimum(first, first + sign * (T - 1)), 0)
        tile = jnp.minimum(lax.shift_right_logical(lowest, 7), CAP // 128 - 4)
        column = 128 * tile + iota((T, 512), 1)
        pick = ones_where((column == first + sign * iota((T, 512), 0)) & (column < cnt))
        found = jnp.concatenate([res[tile + q] for q in range(4)], axis=1)
        return nt(pick, found).astype(BF)

    def tell_count(q, _):
        remote(counts.at[s], counts.at[s], csend.at[0], crecv.at[0], chip(q)).start()
        return 0

    others = pl.ds(0, N_SEQ - 1)
    all_counts = remote(counts.at[others], counts.at[others], csend.at[0], crecv.at[0], chip(1))

    half_c = pl.ds(pl.multiple_of(512 * c, 512), 512)
    sends = []

    def send_edges(m):
        for q, (buffer, where) in enumerate(
            ((send_r, {"seq": right, "ch": 0}), (send_rr, {"seq": left, "ch": 1}))
        ):
            copy = remote(buffer.at[m], edge.at[m, :, half_c], esend.at[m, q], erecv.at[m, c], where)
            copy.start()
            sends.append(copy)

    pl.semaphore_wait(barrier, N_SEQ + 2)
    counts[s] = jnp.full((8, 128), cnt, I32)
    lax.fori_loop(1, N_SEQ, tell_count, 0)
    for copy in load_res:
        copy.wait()
    for i in groups[0]:
        weight_local(i).start()
        sends.append(weight_remote(i))
        sends[-1].start()
    for m in (0, 1):
        send_r[m] = picked(cnt - 1 - T * m, -1)
        send_rr[m] = picked(jnp.int32(T * m), 1)
    for g in (1, 2):
        for i in groups[g]:
            weight_local(i).start()
    all_counts.wait_recv()
    send_edges(0)
    send_edges(1)
    earlier = iota((N_SEQ, 8, 128), 0) < s
    place[...] = jnp.sum(jnp.where(earlier, counts[...], 0), axis=0) - SHARD * s
    offset = place[0, 0]
    gap = jnp.where(c == 0, SHARD // 2 - offset, offset + cnt - SHARD)

    def window(core, n):
        sign = 2 * core - 1
        first = jnp.where(core == 1, 1440, 1631) + sign * T * n - offset
        return picked(first, sign)

    def to_peer(h):
        rows = pl.ds(PAD + EDGE * h, EDGE)
        return remote(shift.at[h], x.at[rows, half_c], hsend.at[h], hrecv.at[h], peer)

    def place_half(h):
        def shifted(n, _):
            shift[h, pl.ds(pl.multiple_of(T * n, 16), T), :] = window(other, 2 * h + n)
            return 0

        lax.fori_loop(0, 2, shifted, 0)
        sends.append(to_peer(h))
        sends[-1].start()

        def placed(n, _):
            x[pl.ds(pl.multiple_of(PAD + EDGE * h + T * n, 16), T), half_c] = window(c, 2 * h + n)
            return 0

        lax.fori_loop(0, 2, placed, 0)

    place_half(0)
    for i in groups[1]:
        sends.append(weight_remote(i))
        sends[-1].start()

    def block(ref, at, rows, b, w, dilation, lag, bound, follow, wide_at):
        here = HEAD - lag

        def tap(j, k):
            def step():
                lanes = pl.ds(512 * k + 256 * j, 256)
                pb[w, HEAD : HEAD + rows, lanes] = nt(a[w, :rows, :], w1[b, lanes, :])

            return step

        def hide(n):
            def step():
                def product(k, start):
                    return pb[w, start : start + rows, pl.ds(512 * k + 128 * n, 128)]

                p0, p1, p2 = product(0, here - dilation), product(1, here), product(2, here + dilation)
                if bound is not None:
                    t = iota((rows, 128), 0) - jnp.where(last, bound, 1 << 20)
                    p0 = jnp.where((t >= 0) & (t < dilation), 0.0, p0)
                    p2 = jnp.where((t < 0) & (t >= -dilation), 0.0, p2)
                hid[w, :rows, pl.ds(128 * n, 128)] = jnp.maximum(p0 + p1 + p2, 0.0).astype(BF)

            return step

        def keep():
            if lag:
                pb[w, 0:HEAD, :] = pb[w, rows : rows + HEAD, :]

        def back(n):
            def step():
                lanes = pl.ds(256 * n, 256)
                update = nt(hid[w, :rows, :], w2[b, lanes, :])
                new = (ref[at : at + rows, lanes].astype(F32) + update).astype(BF)
                ref[at : at + rows, lanes] = new
                if follow is not None:
                    a[follow, :rows, lanes] = jnp.maximum(new, jnp.zeros((), BF))
                if wide_at is not None:
                    for q in (0, 1):
                        y32[2 * n + q, wide_at : wide_at + rows, :] = new[:, 128 * q : 128 * (q + 1)].astype(F32)

            return step

        taps = [tap(j, k) for j in range(2) for k in range(3)]
        return taps, [hide(n) for n in range(4)], [keep] + [back(n) for n in range(4)]

    def beside(*lists):
        longest = max(len(steps) for steps in lists)
        for i in range(longest):
            for steps in lists:
                for step in steps[len(steps) * i // longest : len(steps) * (i + 1) // longest]:
                    step()

    def alone(steps, filler=()):
        taps, hides, backs = steps
        beside(taps[:3], list(filler))
        beside(taps[3:], hides[:2])
        beside(hides[2:])
        beside(backs)

    def pair(first, second):
        beside(first[0])
        beside(second[0], first[1])
        beside(first[2], second[1])
        beside(second[2])

    def half(core):
        return pl.ds(pl.multiple_of(512 * core, 512), 512)

    def own_rows(i, first, count, start):
        rows, to = pl.ds(PAD + first, count), pl.ds(pl.multiple_of(start, 16), count)
        return (
            lambda: pltpu.make_async_copy(x.at[rows, half(c)], out_hbm.at[to], olocal.at[i]),
            lambda: remote(x.at[rows, half(other)], out_hbm.at[to], osend.at[i, 0], opeer.at[i], peer),
        )

    def next_rows(i, first, count):
        return [
            remote(
                x.at[pl.ds(PAD + first, count), pl.ds(512 * core, 512)],
                out_hbm.at[pl.ds(first - EDGE, count)],
                osend.at[i, core],
                oleft.at[i - 2],
                {"seq": right, "ch": core},
            )
            for core in (0, 1)
        ]

    pieces = ((96, 176), (272, 336), (608, 272), (880, 240))

    def emit(i):
        first, count = pieces[i]
        if i < 2:
            for copy in own_rows(i, first, count, jnp.where(c == 0, 416 + first, 1440 + first)):
                copy().start()
        else:

            @pl.when(c == 0)
            def _():
                for copy in own_rows(i, first, count, 416 + first):
                    copy().start()

            @pl.when(c == 1)
            def _():
                for copy in next_rows(i, first, count):
                    copy.start()

    def fold(first, rows):
        def one(n):
            def step():
                for k in range(4):
                    lanes = pl.ds(1024 * k + 128 * n, 128)
                    z[first : first + rows, lanes] = y32[n, pl.ds(4 * first + k, rows, stride=4), :].astype(BF)

            return step

        return [one(n) for n in range(8)]

    def finest(n, b):
        start = PAD + T * n - 16 * b
        bound = EDGE - (T * n - 16 * b - 16) if n == 2 else None
        return block(x, start - 16, T, b, b, (1, 3)[b], 16, bound, None if b else 1, T * n if b else None)

    def ready(n):
        at = PAD + T * n
        if n % 2 == 0:
            to_peer(n // 2).wait_recv()
        if n < 2:
            a[0] = jnp.maximum(x[at : at + T, :], jnp.zeros((), BF))
            return
        m = n - 2
        for core in (0, 1):
            remote(
                send_r.at[m], edge.at[m, :, pl.ds(512 * core, 512)], esend.at[m, 0], erecv.at[m, core],
                {"seq": right, "ch": 0},
            ).wait_recv()
        picks = [ones_where(T * e + iota((T, T), 1) == T * m + iota((T, T), 0) - gap) for e in range(m + 1)]
        for q in range(4):
            lanes = pl.ds(256 * q, 256)
            total = x[at : at + T, lanes].astype(F32)
            for e in range(m + 1):
                total = total + nn(picks[e], edge[e, :, lanes])
            full = total.astype(BF)
            x[at : at + T, lanes] = full
            a[0, :, lanes] = jnp.maximum(full, jnp.zeros((), BF))

    need(block_weights(0))
    ready(0)
    alone(finest(0, 0))
    for i in groups[2]:
        sends.append(weight_remote(i))
        sends[-1].start()
    need(block_weights(1))
    place_half(1)
    for n in range(3):
        ready(n + 1)
        pair(finest(n, 1), finest(n + 1, 0))
        for i in ((0,), (), (1, 2))[n]:
            emit(i)
    alone(finest(3, 1), fold(0, 208))
    emit(3)
    beside(fold(208, T - 208))

    need(down_weights(0))

    def down(l, rows, to):
        for n in range(4):
            lanes = pl.ds(256 * n, 256)
            new = nt(z[:rows, :], dn[l, lanes, :]).astype(BF)
            to[:, lanes] = new
            a[0, :rows, lanes] = jnp.maximum(new, jnp.zeros((), BF))

    down(0, T, u)
    need(block_weights(2))
    need(block_weights(3))
    alone(block(u, 0, T, 2, 0, 1, 0, 160, 1, None))
    alone(block(u, 0, T, 3, 1, 3, 0, 160, None, 0))

    beside(fold(0, T2))
    need(down_weights(1))
    need(block_weights(4))
    down(1, T2, v)
    alone(block(v, 0, T2, 4, 0, 3, 0, 40, None, None))

    need([28])
    load_cb.wait()
    pj[EMB : 2 * EMB, :] = pj[0:EMB, :]
    pj[2 * EMB : 3 * EMB, :] = pj[0:EMB, :]
    book = cb[...]
    book_hi = book.astype(BF)
    cbk[0:EMB, :] = book_hi
    cbk[EMB : 2 * EMB, :] = book_hi
    cbk[2 * EMB : 3 * EMB, :] = (book - book_hi.astype(F32)).astype(BF)
    book_sq = jnp.sum(book * book, axis=0, keepdims=True)
    frame, row = iota((128, T2), 0), iota((128, T2), 1)
    spot = jnp.where(c == 0, 103 - row, lax.rem(88 + row, 128))
    coarse = nn(ones_where((spot == frame) & (row >= 8) & (row < 72)), v[...]).astype(BF)
    latent = nt(pj[0:EMB, :], coarse)
    thrice = nt(coarse, pj[...])
    hi = thrice.astype(BF)
    lo = (thrice - hi.astype(F32)).astype(BF)
    lane = iota((128, 3 * EMB), 1)
    lhs = jnp.where((lane >= EMB) & (lane < 2 * EMB), lo, hi)
    nearest = jnp.full((128, 1), jnp.inf, F32)
    for q in range(4):
        columns = slice(512 * q, 512 * (q + 1))
        distance = book_sq[:, columns] - 2.0 * nn(lhs, cbk[:, columns])
        nearest = jnp.minimum(nearest, jnp.min(distance, axis=1, keepdims=True))
    diagonal = iota((128, 128), 0) == iota((128, 128), 1)
    nearest = jnp.sum(jnp.where(diagonal, nearest, 0.0), axis=0, keepdims=True)
    nearest = (nearest + jnp.sum(latent * latent, axis=0, keepdims=True)) * (1.0 / EMB)
    msg[0:EMB, :] = latent
    msg[EMB : EMB + 8, :] = jnp.broadcast_to(nearest, (8, 128))
    tell_peer = remote(msg, msg_peer, msend.at[0], mrecv.at[0], peer)
    tell_next = [
        remote(msg, msg_left, msend.at[1 + core], mrecv.at[1], {"seq": right, "ch": core}) for core in (0, 1)
    ]
    tell_peer.start()

    @pl.when(c == 1)
    def _():
        for copy in tell_next:
            copy.start()

    tell_peer.wait_recv()
    tell_next[0].wait_recv()
    lane = iota((EMB + 8, 128), 1)
    own = jnp.where(c == 0, msg[...], msg_peer[...])
    late = jnp.where(c == 0, msg_peer[...], msg[...])
    whole = jnp.where(lane < 32, msg_left[...], jnp.where(lane < 96, own, late))
    lat_ref[...] = whole[0:EMB, :]
    near_ref[...] = whole[EMB : EMB + 8, :]

    tell_peer.wait_send()
    for copy in sends:
        copy.wait_send()
    all_counts.wait_send()
    for i in (0, 1):
        first, count = pieces[i]
        mine, theirs = own_rows(i, first, count, jnp.where(c == 0, 416 + first, 1440 + first))
        mine().wait()
        theirs().wait()
        next_rows(2 + i, *pieces[2 + i])[0].wait_recv()

    @pl.when(c == 0)
    def _():
        for i in (2, 3):
            mine, theirs = own_rows(i, *pieces[i], 416 + pieces[i][0])
            mine().wait()
            theirs().wait_send()

    @pl.when(c == 1)
    def _():
        for copy in tell_next:
            copy.wait_send()
        for i in (2, 3):
            own_rows(i, *pieces[i], 416 + pieces[i][0])[1]().wait_recv()
            for copy in next_rows(i, *pieces[i]):
                copy.wait_send()


def hand_over(frames, latent, nearest, sharpest_out, latent_out, nearest_out, rows, columns, sem):
    def read(j):
        return pltpu.make_async_copy(frames.at[pl.ds(256 * j, 256)], rows.at[j], sem.at[0, j])

    def write(j):
        return pltpu.make_async_copy(columns.at[j], sharpest_out.at[:, pl.ds(256 * j, 256)], sem.at[1, j])

    for j in range(8):
        read(j).start()
    latent_out[...] = latent[...]
    nearest_out[...] = nearest[0]
    r, q = iota((256, 256), 0), iota((256, 256), 1)
    same, reverse = ones_where(r == q), ones_where(255 - r == q)
    for j in range(8):
        read(j).wait()

    def turned(j, to):
        for h in (0, 1):
            part = rows[j, :, 256 * h : 256 * (h + 1)]
            if to != j:
                part = nn(reverse, part).astype(BF)
            columns[to, 256 * h : 256 * (h + 1), :] = nt(same, part).astype(BF)

    for group in ((0, 1, 6, 7), (2, 3, 4, 5)):
        for j in group:
            turned(j, 7 - j if 2 <= j < 6 else j)
        for j in group:
            write(j).start()
    for j in range(8):
        write(j).wait()


def on_device(samples, sample_counts, spaced, restore, shrinking, projector, dictionary):
    hbm = pl.BlockSpec(memory_space=pltpu.HBM)
    vmem = pl.BlockSpec(memory_space=pltpu.VMEM)
    dma = pltpu.SemaphoreType.DMA
    frames, latent, nearest = pl.pallas_call(
        kernel,
        out_shape=(
            jax.ShapeDtypeStruct((SHARD, H), BF),
            jax.ShapeDtypeStruct((EMB, 128), F32),
            jax.ShapeDtypeStruct((8, 128), F32),
        ),
        in_specs=[pl.BlockSpec(memory_space=pltpu.SMEM)] + [hbm] * 6,
        out_specs=(hbm, vmem, vmem),
        scratch_shapes=[
            pltpu.VMEM((CAP // 128, H, 128), BF),
            pltpu.VMEM((5, 3 * H, C), BF),
            pltpu.VMEM((5, C, H), BF),
            pltpu.VMEM((2, C, 4 * C), BF),
            pltpu.VMEM((3 * EMB, C), BF),
            pltpu.VMEM((EMB, BINS), F32),
            pltpu.VMEM((3 * EMB, BINS), BF),
            pltpu.VMEM((N_SEQ, 8, 128), I32),
            pltpu.VMEM((8, 128), I32),
            pltpu.VMEM((2, T, C), BF),
            pltpu.VMEM((2, T, H), BF),
            pltpu.VMEM((2, T, H), BF),
            pltpu.VMEM((2, EDGE, H), BF),
            pltpu.VMEM((PAD + 4 * T, C), BF),
            pltpu.VMEM((2, T, C), BF),
            pltpu.VMEM((2, HEAD + T + 8, 3 * H), F32),
            pltpu.VMEM((2, T, H), BF),
            pltpu.VMEM((8, 4 * T, 128), F32),
            pltpu.VMEM((T, 4 * C), BF),
            pltpu.VMEM((T, C), BF),
            pltpu.VMEM((T2, C), BF),
            pltpu.VMEM((EMB + 8, 128), F32),
            pltpu.VMEM((EMB + 8, 128), F32),
            pltpu.VMEM((EMB + 8, 128), F32),
            dma((31,)),
            dma((CAP // 128,)),
            dma((29,)),
            dma((29,)),
            dma((1,)),
            dma((1,)),
            dma((2, 2)),
            dma((2, 2)),
            dma((2,)),
            dma((2,)),
            dma((4,)),
            dma((4, 2)),
            dma((4,)),
            dma((2,)),
            dma((3,)),
            dma((2,)),
        ],
        compiler_params=pltpu.CompilerParams(
            collective_id=0, has_side_effects=True, vmem_limit_bytes=63 * 2**20
        ),
        name="encoder",
    )(sample_counts, samples, spaced, restore, shrinking, projector, dictionary)
    return pl.pallas_call(
        hand_over,
        out_shape=(
            jax.ShapeDtypeStruct((H, SHARD), BF),
            jax.ShapeDtypeStruct((EMB, 128), F32),
            jax.ShapeDtypeStruct((128,), F32),
        ),
        in_specs=[hbm, vmem, vmem],
        out_specs=(hbm, vmem, vmem),
        scratch_shapes=[pltpu.VMEM((8, 256, H), BF), pltpu.VMEM((8, H, 256), BF), dma((2, 8))],
        name="hand_over",
    )(frames, latent, nearest)


def solution(mesh):
    return jax.shard_map(
        on_device,
        mesh=mesh,
        in_specs=(
            P("ch", "seq"),
            P("seq"),
            P(None, None, "ch", None),
            P(None, None, "ch"),
            P(None, None, "ch", None),
            P(None, "ch"),
            P(),
        ),
        out_specs=(P("ch", "seq"), P(None, "seq"), P("seq")),
        check_vma=False,
    )
```

```python
import jax
import jax.numpy as jnp
from jax import lax
from jax.experimental import pallas as pl
from jax.experimental.pallas import tpu as pltpu
from jax.sharding import PartitionSpec as P

MESH = pl.DeviceIdType.MESH
BF, F32, I32 = jnp.bfloat16, jnp.float32, jnp.int32
C, H, EMB, BINS, SHARD, CAP = 1024, 512, 64, 2048, 2048, 3072
T = 304
T2 = 80
N_SEQ = 64
HEAD = 24
PAD = 32
EDGE = 2 * T


def nt(a, b):
    return lax.dot_general(a, b, (((1,), (1,)), ((), ())), preferred_element_type=F32)


def nn(a, b):
    return jnp.dot(a, b, preferred_element_type=F32)


def iota(shape, dim):
    return lax.broadcasted_iota(I32, shape, dim)


def ones_where(mask):
    return jnp.where(mask, 1.0, 0.0).astype(BF)


def kernel(
    cnt_ref, res_hbm, w1_hbm, w2_hbm, dn_hbm, pj_hbm, cb_hbm,
    out_hbm, lat_ref, near_ref,
    res, w1, w2, dn, pj, cb, cbk, counts, place, edge, send_r, send_rr, shift, x, a, pb, hid, y32, z, u, v,
    msg, msg_peer, msg_left,
    lsem, rsem, wsend, wrecv, csend, crecv, esend, erecv, hsend, hrecv, olocal, osend, opeer, oleft, msend, mrecv,
):
    s, c = lax.axis_index("seq"), lax.axis_index("ch")
    n_seq = lax.axis_size("seq")
    right, left = lax.rem(s + 1, n_seq), lax.rem(s + n_seq - 1, n_seq)
    other = 1 - c
    peer = {"seq": s, "ch": other}
    last = (s == n_seq - 1) & (c == 1)

    def remote(src, dst, send, recv, where):
        return pltpu.make_async_remote_copy(
            src_ref=src, dst_ref=dst, send_sem=send, recv_sem=recv, device_id=where, device_id_type=MESH
        )

    def weight(i, on):
        if i < 15:
            b, k = divmod(i, 3)
            tap = k + (1 - on) * (2 - 2 * k)
            return w1_hbm.at[b, k], w1.at[b, pl.ds(pl.multiple_of(512 * tap + 256 * c, 256), 256)]
        if i < 20:
            return w2_hbm.at[i - 15], w2.at[i - 15, :, pl.ds(pl.multiple_of(256 * c, 256), 256)]
        if i < 28:
            l, k = divmod(i - 20, 4)
            tap = k + (1 - on) * (3 - 2 * k)
            return dn_hbm.at[l, k], dn.at[
                l, pl.ds(pl.multiple_of(512 * c, 512), 512), pl.ds(pl.multiple_of(1024 * tap, 1024), 1024)
            ]
        return pj_hbm, pj.at[pl.ds(0, EMB), pl.ds(pl.multiple_of(512 * c, 512), 512)]

    def weight_local(i):
        return pltpu.make_async_copy(*weight(i, c), lsem.at[i])

    def weight_remote(i):
        return remote(*weight(i, other), wsend.at[i], wrecv.at[i], peer)

    def block_weights(b):
        return [3 * b, 3 * b + 1, 3 * b + 2, 15 + b]

    def down_weights(l):
        return [20 + 4 * l + k for k in range(4)]

    def need(items):
        for i in items:
            weight_local(i).wait()
            weight_remote(i).wait_recv()

    groups = [
        block_weights(0) + block_weights(1),
        down_weights(0) + block_weights(2),
        block_weights(3) + down_weights(1) + block_weights(4) + [28],
    ]
    load_res = [
        pltpu.make_async_copy(res_hbm.at[:, pl.ds(128 * k, 128)], res.at[k], rsem.at[k]) for k in range(CAP // 128)
    ]
    load_cb = pltpu.make_async_copy(cb_hbm, cb, lsem.at[30])
    barrier = pltpu.get_barrier_semaphore()
    def chip(q):
        return {"seq": lax.rem(s + q, n_seq), "ch": c}

    def greet(q, _):
        pl.semaphore_signal(barrier, inc=1, device_id=chip(q), device_id_type=MESH)
        return 0

    lax.fori_loop(1, N_SEQ, greet, 0)
    for where in (peer, {"seq": left, "ch": other}, {"seq": right, "ch": other}):
        pl.semaphore_signal(barrier, inc=1, device_id=where, device_id_type=MESH)
    for copy in load_res:
        copy.start()
    load_cb.start()

    cnt = cnt_ref[0]
    x[0:PAD, :] = jnp.zeros((PAD, C), BF)
    for w in (0, 1):
        pb[w, 0:HEAD, :] = jnp.zeros((HEAD, 3 * H), F32)
        pb[w, HEAD + T :, :] = jnp.zeros((8, 3 * H), F32)

    def picked(first, sign):
        lowest = jnp.maximum(jnp.minimum(first, first + sign * (T - 1)), 0)
        tile = jnp.minimum(lax.shift_right_logical(lowest, 7), CAP // 128 - 4)
        column = 128 * tile + iota((T, 512), 1)
        pick = ones_where((column == first + sign * iota((T, 512), 0)) & (column < cnt))
        found = jnp.concatenate([res[tile + q] for q in range(4)], axis=1)
        return nt(pick, found).astype(BF)

    def tell_count(q, _):
        remote(counts.at[s], counts.at[s], csend.at[0], crecv.at[0], chip(q)).start()
        return 0

    others = pl.ds(0, N_SEQ - 1)
    all_counts = remote(counts.at[others], counts.at[others], csend.at[0], crecv.at[0], chip(1))

    half_c = pl.ds(pl.multiple_of(512 * c, 512), 512)
    sends = []

    def send_edges(m):
        for q, (buffer, where) in enumerate(
            ((send_r, {"seq": right, "ch": 0}), (send_rr, {"seq": left, "ch": 1}))
        ):
            copy = remote(buffer.at[m], edge.at[m, :, half_c], esend.at[m, q], erecv.at[m, c], where)
            copy.start()
            sends.append(copy)

    pl.semaphore_wait(barrier, N_SEQ + 2)
    counts[s] = jnp.full((8, 128), cnt, I32)
    lax.fori_loop(1, N_SEQ, tell_count, 0)
    for copy in load_res:
        copy.wait()
    for i in groups[0]:
        weight_local(i).start()
        sends.append(weight_remote(i))
        sends[-1].start()
    for m in (0, 1):
        send_r[m] = picked(cnt - 1 - T * m, -1)
        send_rr[m] = picked(jnp.int32(T * m), 1)
    for g in (1, 2):
        for i in groups[g]:
            weight_local(i).start()
    all_counts.wait_recv()
    send_edges(0)
    send_edges(1)
    earlier = iota((N_SEQ, 8, 128), 0) < s
    place[...] = jnp.sum(jnp.where(earlier, counts[...], 0), axis=0) - SHARD * s
    offset = place[0, 0]
    gap = jnp.where(c == 0, SHARD // 2 - offset, offset + cnt - SHARD)

    def window(core, n):
        sign = 2 * core - 1
        first = jnp.where(core == 1, 1440, 1631) + sign * T * n - offset
        return picked(first, sign)

    def to_peer(h):
        rows = pl.ds(PAD + EDGE * h, EDGE)
        return remote(shift.at[h], x.at[rows, half_c], hsend.at[h], hrecv.at[h], peer)

    def place_half(h):
        def shifted(n, _):
            shift[h, pl.ds(pl.multiple_of(T * n, 16), T), :] = window(other, 2 * h + n)
            return 0

        lax.fori_loop(0, 2, shifted, 0)
        sends.append(to_peer(h))
        sends[-1].start()

        def placed(n, _):
            x[pl.ds(pl.multiple_of(PAD + EDGE * h + T * n, 16), T), half_c] = window(c, 2 * h + n)
            return 0

        lax.fori_loop(0, 2, placed, 0)

    place_half(0)
    for i in groups[1]:
        sends.append(weight_remote(i))
        sends[-1].start()

    def block(ref, at, rows, b, w, dilation, lag, bound, follow, wide_at):
        here = HEAD - lag

        def tap(j, k):
            def step():
                lanes = pl.ds(512 * k + 256 * j, 256)
                pb[w, HEAD : HEAD + rows, lanes] = nt(a[w, :rows, :], w1[b, lanes, :])

            return step

        def hide(n):
            def step():
                def product(k, start):
                    return pb[w, start : start + rows, pl.ds(512 * k + 128 * n, 128)]

                p0, p1, p2 = product(0, here - dilation), product(1, here), product(2, here + dilation)
                if bound is not None:
                    t = iota((rows, 128), 0) - jnp.where(last, bound, 1 << 20)
                    p0 = jnp.where((t >= 0) & (t < dilation), 0.0, p0)
                    p2 = jnp.where((t < 0) & (t >= -dilation), 0.0, p2)
                hid[w, :rows, pl.ds(128 * n, 128)] = jnp.maximum(p0 + p1 + p2, 0.0).astype(BF)

            return step

        def keep():
            if lag:
                pb[w, 0:HEAD, :] = pb[w, rows : rows + HEAD, :]

        def back(n):
            def step():
                lanes = pl.ds(256 * n, 256)
                update = nt(hid[w, :rows, :], w2[b, lanes, :])
                new = (ref[at : at + rows, lanes].astype(F32) + update).astype(BF)
                ref[at : at + rows, lanes] = new
                if follow is not None:
                    a[follow, :rows, lanes] = jnp.maximum(new, jnp.zeros((), BF))
                if wide_at is not None:
                    for q in (0, 1):
                        y32[2 * n + q, wide_at : wide_at + rows, :] = new[:, 128 * q : 128 * (q + 1)].astype(F32)

            return step

        taps = [tap(j, k) for j in range(2) for k in range(3)]
        return taps, [hide(n) for n in range(4)], [keep] + [back(n) for n in range(4)]

    def beside(*lists):
        longest = max(len(steps) for steps in lists)
        for i in range(longest):
            for steps in lists:
                for step in steps[len(steps) * i // longest : len(steps) * (i + 1) // longest]:
                    step()

    def alone(steps, filler=()):
        taps, hides, backs = steps
        beside(taps[:3], list(filler))
        beside(taps[3:], hides[:2])
        beside(hides[2:])
        beside(backs)

    def pair(first, second):
        beside(first[0])
        beside(second[0], first[1])
        beside(first[2], second[1])
        beside(second[2])

    def half(core):
        return pl.ds(pl.multiple_of(512 * core, 512), 512)

    def own_rows(i, first, count, start):
        rows, to = pl.ds(PAD + first, count), pl.ds(pl.multiple_of(start, 16), count)
        return (
            lambda: pltpu.make_async_copy(x.at[rows, half(c)], out_hbm.at[to], olocal.at[i]),
            lambda: remote(x.at[rows, half(other)], out_hbm.at[to], osend.at[i, 0], opeer.at[i], peer),
        )

    def next_rows(i, first, count):
        return [
            remote(
                x.at[pl.ds(PAD + first, count), pl.ds(512 * core, 512)],
                out_hbm.at[pl.ds(first - EDGE, count)],
                osend.at[i, core],
                oleft.at[i - 2],
                {"seq": right, "ch": core},
            )
            for core in (0, 1)
        ]

    pieces = ((96, 176), (272, 336), (608, 272), (880, 240))

    def emit(i):
        first, count = pieces[i]
        if i < 2:
            for copy in own_rows(i, first, count, jnp.where(c == 0, 416 + first, 1440 + first)):
                copy().start()
        else:

            @pl.when(c == 0)
            def _():
                for copy in own_rows(i, first, count, 416 + first):
                    copy().start()

            @pl.when(c == 1)
            def _():
                for copy in next_rows(i, first, count):
                    copy.start()

    def fold(first, rows):
        def one(n):
            def step():
                for k in range(4):
                    lanes = pl.ds(1024 * k + 128 * n, 128)
                    z[first : first + rows, lanes] = y32[n, pl.ds(4 * first + k, rows, stride=4), :].astype(BF)

            return step

        return [one(n) for n in range(8)]

    def finest(n, b):
        start = PAD + T * n - 16 * b
        bound = EDGE - (T * n - 16 * b - 16) if n == 2 else None
        return block(x, start - 16, T, b, b, (1, 3)[b], 16, bound, None if b else 1, T * n if b else None)

    def ready(n):
        at = PAD + T * n
        if n % 2 == 0:
            to_peer(n // 2).wait_recv()
        if n < 2:
            a[0] = jnp.maximum(x[at : at + T, :], jnp.zeros((), BF))
            return
        m = n - 2
        for core in (0, 1):
            remote(
                send_r.at[m], edge.at[m, :, pl.ds(512 * core, 512)], esend.at[m, 0], erecv.at[m, core],
                {"seq": right, "ch": 0},
            ).wait_recv()
        picks = [ones_where(T * e + iota((T, T), 1) == T * m + iota((T, T), 0) - gap) for e in range(m + 1)]
        for q in range(4):
            lanes = pl.ds(256 * q, 256)
            total = x[at : at + T, lanes].astype(F32)
            for e in range(m + 1):
                total = total + nn(picks[e], edge[e, :, lanes])
            full = total.astype(BF)
            x[at : at + T, lanes] = full
            a[0, :, lanes] = jnp.maximum(full, jnp.zeros((), BF))

    need(block_weights(0))
    ready(0)
    alone(finest(0, 0))
    for i in groups[2]:
        sends.append(weight_remote(i))
        sends[-1].start()
    need(block_weights(1))
    place_half(1)
    for n in range(3):
        ready(n + 1)
        pair(finest(n, 1), finest(n + 1, 0))
        for i in ((0,), (), (1, 2))[n]:
            emit(i)
    alone(finest(3, 1), fold(0, 208))
    emit(3)
    beside(fold(208, T - 208))

    need(down_weights(0))

    def down(l, rows, to):
        for n in range(4):
            lanes = pl.ds(256 * n, 256)
            new = nt(z[:rows, :], dn[l, lanes, :]).astype(BF)
            to[:, lanes] = new
            a[0, :rows, lanes] = jnp.maximum(new, jnp.zeros((), BF))

    down(0, T, u)
    need(block_weights(2))
    need(block_weights(3))
    alone(block(u, 0, T, 2, 0, 1, 0, 160, 1, None))
    alone(block(u, 0, T, 3, 1, 3, 0, 160, None, 0))

    beside(fold(0, T2))
    need(down_weights(1))
    need(block_weights(4))
    down(1, T2, v)
    alone(block(v, 0, T2, 4, 0, 3, 0, 40, None, None))

    need([28])
    load_cb.wait()
    pj[EMB : 2 * EMB, :] = pj[0:EMB, :]
    pj[2 * EMB : 3 * EMB, :] = pj[0:EMB, :]
    book = cb[...]
    book_hi = book.astype(BF)
    cbk[0:EMB, :] = book_hi
    cbk[EMB : 2 * EMB, :] = book_hi
    cbk[2 * EMB : 3 * EMB, :] = (book - book_hi.astype(F32)).astype(BF)
    book_sq = jnp.sum(book * book, axis=0, keepdims=True)
    frame, row = iota((128, T2), 0), iota((128, T2), 1)
    spot = jnp.where(c == 0, 103 - row, lax.rem(88 + row, 128))
    coarse = nn(ones_where((spot == frame) & (row >= 8) & (row < 72)), v[...]).astype(BF)
    latent = nt(pj[0:EMB, :], coarse)
    thrice = nt(coarse, pj[...])
    hi = thrice.astype(BF)
    lo = (thrice - hi.astype(F32)).astype(BF)
    lane = iota((128, 3 * EMB), 1)
    lhs = jnp.where((lane >= EMB) & (lane < 2 * EMB), lo, hi)
    nearest = jnp.full((128, 1), jnp.inf, F32)
    for q in range(4):
        columns = slice(512 * q, 512 * (q + 1))
        distance = book_sq[:, columns] - 2.0 * nn(lhs, cbk[:, columns])
        nearest = jnp.minimum(nearest, jnp.min(distance, axis=1, keepdims=True))
    diagonal = iota((128, 128), 0) == iota((128, 128), 1)
    nearest = jnp.sum(jnp.where(diagonal, nearest, 0.0), axis=0, keepdims=True)
    nearest = (nearest + jnp.sum(latent * latent, axis=0, keepdims=True)) * (1.0 / EMB)
    msg[0:EMB, :] = latent
    msg[EMB : EMB + 8, :] = jnp.broadcast_to(nearest, (8, 128))
    tell_peer = remote(msg, msg_peer, msend.at[0], mrecv.at[0], peer)
    tell_next = [
        remote(msg, msg_left, msend.at[1 + core], mrecv.at[1], {"seq": right, "ch": core}) for core in (0, 1)
    ]
    tell_peer.start()

    @pl.when(c == 1)
    def _():
        for copy in tell_next:
            copy.start()

    tell_peer.wait_recv()
    tell_next[0].wait_recv()
    lane = iota((EMB + 8, 128), 1)
    own = jnp.where(c == 0, msg[...], msg_peer[...])
    late = jnp.where(c == 0, msg_peer[...], msg[...])
    whole = jnp.where(lane < 32, msg_left[...], jnp.where(lane < 96, own, late))
    lat_ref[...] = whole[0:EMB, :]
    near_ref[...] = whole[EMB : EMB + 8, :]

    tell_peer.wait_send()
    for copy in sends:
        copy.wait_send()
    all_counts.wait_send()
    for i in (0, 1):
        first, count = pieces[i]
        mine, theirs = own_rows(i, first, count, jnp.where(c == 0, 416 + first, 1440 + first))
        mine().wait()
        theirs().wait()
        next_rows(2 + i, *pieces[2 + i])[0].wait_recv()

    @pl.when(c == 0)
    def _():
        for i in (2, 3):
            mine, theirs = own_rows(i, *pieces[i], 416 + pieces[i][0])
            mine().wait()
            theirs().wait_send()

    @pl.when(c == 1)
    def _():
        for copy in tell_next:
            copy.wait_send()
        for i in (2, 3):
            own_rows(i, *pieces[i], 416 + pieces[i][0])[1]().wait_recv()
            for copy in next_rows(i, *pieces[i]):
                copy.wait_send()


def hand_over(frames, latent, nearest, sharpest_out, latent_out, nearest_out, rows, columns, sem):
    def read(j):
        return pltpu.make_async_copy(frames.at[pl.ds(256 * j, 256)], rows.at[j], sem.at[0, j])

    def write(j):
        return pltpu.make_async_copy(columns.at[j], sharpest_out.at[:, pl.ds(256 * j, 256)], sem.at[1, j])

    for j in (0, 1, 6, 7, 2, 3, 4, 5):
        read(j).start()
    latent_out[...] = latent[...]
    nearest_out[...] = nearest[0]
    r, q = iota((256, 256), 0), iota((256, 256), 1)
    same, reverse = ones_where(r == q), ones_where(255 - r == q)
    def turned(j, to):
        for h in (0, 1):
            part = rows[j, :, 256 * h : 256 * (h + 1)]
            if to != j:
                part = nn(reverse, part).astype(BF)
            columns[to, 256 * h : 256 * (h + 1), :] = nt(same, part).astype(BF)

    for group in ((0, 1, 6, 7), (2, 3, 4, 5)):
        for j in group:
            read(j).wait()
        for j in group:
            turned(j, 7 - j if 2 <= j < 6 else j)
        for j in group:
            write(j).start()
    for j in range(8):
        write(j).wait()


def on_device(samples, sample_counts, spaced, restore, shrinking, projector, dictionary):
    hbm = pl.BlockSpec(memory_space=pltpu.HBM)
    vmem = pl.BlockSpec(memory_space=pltpu.VMEM)
    dma = pltpu.SemaphoreType.DMA
    frames, latent, nearest = pl.pallas_call(
        kernel,
        out_shape=(
            jax.ShapeDtypeStruct((SHARD, H), BF),
            jax.ShapeDtypeStruct((EMB, 128), F32),
            jax.ShapeDtypeStruct((8, 128), F32),
        ),
        in_specs=[pl.BlockSpec(memory_space=pltpu.SMEM)] + [hbm] * 6,
        out_specs=(hbm, vmem, vmem),
        scratch_shapes=[
            pltpu.VMEM((CAP // 128, H, 128), BF),
            pltpu.VMEM((5, 3 * H, C), BF),
            pltpu.VMEM((5, C, H), BF),
            pltpu.VMEM((2, C, 4 * C), BF),
            pltpu.VMEM((3 * EMB, C), BF),
            pltpu.VMEM((EMB, BINS), F32),
            pltpu.VMEM((3 * EMB, BINS), BF),
            pltpu.VMEM((N_SEQ, 8, 128), I32),
            pltpu.VMEM((8, 128), I32),
            pltpu.VMEM((2, T, C), BF),
            pltpu.VMEM((2, T, H), BF),
            pltpu.VMEM((2, T, H), BF),
            pltpu.VMEM((2, EDGE, H), BF),
            pltpu.VMEM((PAD + 4 * T, C), BF),
            pltpu.VMEM((2, T, C), BF),
            pltpu.VMEM((2, HEAD + T + 8, 3 * H), F32),
            pltpu.VMEM((2, T, H), BF),
            pltpu.VMEM((8, 4 * T, 128), F32),
            pltpu.VMEM((T, 4 * C), BF),
            pltpu.VMEM((T, C), BF),
            pltpu.VMEM((T2, C), BF),
            pltpu.VMEM((EMB + 8, 128), F32),
            pltpu.VMEM((EMB + 8, 128), F32),
            pltpu.VMEM((EMB + 8, 128), F32),
            dma((31,)),
            dma((CAP // 128,)),
            dma((29,)),
            dma((29,)),
            dma((1,)),
            dma((1,)),
            dma((2, 2)),
            dma((2, 2)),
            dma((2,)),
            dma((2,)),
            dma((4,)),
            dma((4, 2)),
            dma((4,)),
            dma((2,)),
            dma((3,)),
            dma((2,)),
        ],
        compiler_params=pltpu.CompilerParams(
            collective_id=0, has_side_effects=True, vmem_limit_bytes=63 * 2**20
        ),
        name="encoder",
    )(sample_counts, samples, spaced, restore, shrinking, projector, dictionary)
    return pl.pallas_call(
        hand_over,
        out_shape=(
            jax.ShapeDtypeStruct((H, SHARD), BF),
            jax.ShapeDtypeStruct((EMB, 128), F32),
            jax.ShapeDtypeStruct((128,), F32),
        ),
        in_specs=[hbm, vmem, vmem],
        out_specs=(hbm, vmem, vmem),
        scratch_shapes=[pltpu.VMEM((8, 256, H), BF), pltpu.VMEM((8, H, 256), BF), dma((2, 8))],
        name="hand_over",
    )(frames, latent, nearest)


def solution(mesh):
    return jax.shard_map(
        on_device,
        mesh=mesh,
        in_specs=(
            P("ch", "seq"),
            P("seq"),
            P(None, None, "ch", None),
            P(None, None, "ch"),
            P(None, None, "ch", None),
            P(None, "ch"),
            P(),
        ),
        out_specs=(P("ch", "seq"), P(None, "seq"), P("seq")),
        check_vma=False,
    )
```
